256 devices in a mesh: row: 8 (over x, z_lo), col: 32 (over y, z_hi, core).
Axes of the slice: x: 4, y: 4, z: 8 (z_hi: 4, z_lo: 2; z = z_hi * 2 + z_lo), core: 2. Of those that a mesh axis runs over, the one named last changes fastest.
Arguments:
- features: bfloat16 [262144, 128], P(('row', 'col')), may hold values from -6 to 6
- tiles: bfloat16 [8, 32, 368, 128, 128], P('row', 'col'), may hold values from -0.078125 to 0.078125
- tile_rows: int32 [8, 32, 368], P('row', 'col'), may hold values from 0 to 255
- tile_cols: int32 [8, 32, 368], P('row', 'col'), may hold values from 0 to 63
- tile_count: int32 [8, 32], P('row', 'col'), may hold values from 92 to 368, as said below
- weight: bfloat16 [128, 128], replicated, may hold values from -0.5 to 0.5
- bias: float32 [128], replicated, may hold values from -3 to 3
- cotangent: bfloat16 [262144, 128], P(('row', 'col')), may hold values from -6 to 6
Outputs:
- activations: bfloat16 [262144, 128], P(('row', 'col'))
- grad_features: bfloat16 [262144, 128], P(('row', 'col'))
- grad_weight: float32 [128, 128], replicated
- grad_bias: float32 [128], replicated
The draws below stay inside these ranges and needn't reach their ends.
Inputs may be any that keep to these rules, and one draw needn't show every extreme that they name: `tile_count`: live slots of one grid cell; some cell has all 368 live.
All inputs are finite; a program needn't handle non-finite values.
Results may differ from the reference program's by a relative error of at most 0.0059.
Values may be sent and summed in bfloat16 or wider, within the bound.
No kernel may reach another device: no remote copies, remote signals or barrier semaphores. Data moves between devices by JAX's collectives and lax.ppermute only.
A program may use at most 128 MiB of HBM per device.

```python
import jax
import jax.numpy as jnp
from jax import lax

F = 128
TILE = 128
SHARD = 1024
TMAX = 368
NODES = 262144
N_ROW = 8
N_COL = 32


def draw_tile_count(key, part):
    key = jax.random.fold_in(key, 11)
    first, second = jax.random.split(key)
    counts = jax.random.randint(first, (N_ROW * N_COL,), TMAX // 4, TMAX + 1)
    chosen = jax.random.randint(second, (), 0, N_ROW * N_COL)
    counts = jnp.where(jnp.arange(N_ROW * N_COL) == chosen, TMAX, counts)
    return counts.reshape(N_ROW, N_COL).astype(jnp.int32)


def with_ends(drawn, own_key, least, high):
    index_at = [jax.random.randint(jax.random.fold_in(own_key, axis), (), 0, length) for axis, length in enumerate(drawn.shape)]
    widest = drawn.shape.index(max(drawn.shape))
    beside = index_at[:widest] + [(index_at[widest] + 1) % drawn.shape[widest]] + index_at[widest + 1:]
    return drawn.at[tuple(index_at)].set(least).at[tuple(beside)].set(high)


def levels(stream_key, shape, shards, least, top_value):
    def one(axis_at, blocks):
        steps = jax.random.uniform(jax.random.fold_in(jax.random.fold_in(stream_key, 6), axis_at), (blocks,), jnp.float32, least / len(shards), top_value / len(shards))
        return jnp.repeat(jnp.exp(steps), shape[axis_at] // blocks).reshape((-1,) + (1,) * (len(shape) - axis_at - 1))

    gain = one(*shards[0])
    for cut in shards[1:]:
        gain = gain * one(*cut)
    return gain


def gaussian(stream_key, extent, width, bound, cuts=(), held_as=jnp.bfloat16):
    loudness = levels(stream_key, extent, cuts, -0.22, 0.18) if cuts else 1.0
    drawn = jax.random.normal(stream_key, extent, jnp.float32) * width * loudness
    return jnp.minimum(jnp.maximum(drawn, -bound), bound).astype(held_as)


def setup_inputs(seed: int = 0) -> dict:
    streams_of = jax.random.split(jax.random.key(seed), 9)
    features = gaussian(streams_of[0], (NODES, F), 1.0, 6.0, ((0, 256),))
    tiles = gaussian(streams_of[1], (N_ROW, N_COL, TMAX, TILE, TILE), (TMAX * TILE * TILE // SHARD) ** -0.5, 0.078125, ((0, 8), (1, 32)))
    tile_rows = with_ends(jax.random.randint(streams_of[2], (N_ROW, N_COL, TMAX), 0, N_COL * SHARD // TILE), jax.random.fold_in(streams_of[2], 1), 0, (N_COL * SHARD // TILE) - 1).astype(jnp.int32)
    tile_cols = with_ends(jax.random.randint(streams_of[3], (N_ROW, N_COL, TMAX), 0, N_ROW * SHARD // TILE), jax.random.fold_in(streams_of[3], 1), 0, (N_ROW * SHARD // TILE) - 1).astype(jnp.int32)
    tile_count = draw_tile_count(jax.random.fold_in(streams_of[8], 71), 0)
    weight = gaussian(streams_of[5], (F, F), F ** -0.5, 0.5)
    bias = gaussian(streams_of[6], (F,), 0.5, 3.0, (), jnp.float32)
    cotangent = gaussian(streams_of[7], (NODES, F), 1.0, 6.0, ((0, 256),))
    return {"features": features, "tiles": tiles, "tile_rows": tile_rows, "tile_cols": tile_cols, "tile_count": tile_count, "weight": weight, "bias": bias, "cotangent": cotangent}


def aggregate_ref(tile_set, dest, source, count, blocks, segments, flip):
    live_slots = jnp.arange(tile_set.shape[0], dtype=jnp.int32) < count
    picked = blocks[source].astype(jnp.float32)
    values = tile_set.astype(jnp.float32)
    if flip:
        product = jnp.einsum('tji,tjf->tif', values, picked)
    else:
        product = jnp.einsum('tij,tjf->tif', values, picked)
    product = jnp.where(live_slots[:, None, None], product, jnp.float32(0.0))
    return jax.ops.segment_sum(product, dest, num_segments=segments)


def reference(features, tiles, tile_rows, tile_cols, tile_count, weight, bias, cotangent):
    row_tiles = N_COL * SHARD // TILE
    col_tiles = N_ROW * SHARD // TILE
    grouped = features.reshape(N_ROW, N_COL, SHARD, F)

    def forward_cell(carry, index):
        rowpos = index // N_COL
        colpos = index % N_COL
        blocks = grouped[:, colpos].reshape(col_tiles, TILE, F)
        part = aggregate_ref(tiles[rowpos, colpos], tile_rows[rowpos, colpos], tile_cols[rowpos, colpos], tile_count[rowpos, colpos], blocks, row_tiles, False)
        return carry.at[rowpos].add(part), None

    start_rows = jnp.zeros((N_ROW, row_tiles, TILE, F), jnp.float32)
    summed, _ = lax.scan(forward_cell, start_rows, jnp.arange(N_ROW * N_COL, dtype=jnp.int32))
    hidden = summed.reshape(NODES, F).astype(jnp.bfloat16)
    pre = jnp.dot(hidden, weight, preferred_element_type=jnp.float32) + bias
    activations = jax.nn.silu(pre).astype(jnp.bfloat16)
    sigma = jax.nn.sigmoid(pre)
    grad_pre = cotangent.astype(jnp.float32) * sigma * (1.0 + pre * (1.0 - sigma))
    grad_bias = jnp.sum(grad_pre, axis=0)
    grad_round = grad_pre.astype(jnp.bfloat16)
    grad_weight = jnp.dot(hidden.T, grad_round, preferred_element_type=jnp.float32)
    grad_hidden = jnp.dot(grad_round, weight.T, preferred_element_type=jnp.float32).astype(jnp.bfloat16)
    hidden_groups = grad_hidden.reshape(N_ROW, row_tiles, TILE, F)

    def backward_cell(carry, index):
        rowpos = index // N_COL
        colpos = index % N_COL
        part = aggregate_ref(tiles[rowpos, colpos], tile_cols[rowpos, colpos], tile_rows[rowpos, colpos], tile_count[rowpos, colpos], hidden_groups[rowpos], col_tiles, True)
        return carry.at[colpos].add(part), None

    start_cols = jnp.zeros((N_COL, col_tiles, TILE, F), jnp.float32)
    back, _ = lax.scan(backward_cell, start_cols, jnp.arange(N_ROW * N_COL, dtype=jnp.int32))
    grad_features = back.reshape(N_COL, N_ROW, SHARD, F).transpose(1, 0, 2, 3).reshape(NODES, F).astype(jnp.bfloat16)
    return activations, grad_features, grad_weight, grad_bias
```

```python
import functools

import jax
import jax.numpy as jnp
from jax import lax
from jax.experimental import pallas as pl
from jax.experimental.pallas import tpu as pltpu
from jax.sharding import PartitionSpec as P

NX, NZL, NY, NZH, NCO = 4, 2, 4, 4, 2
EDGE = 128
CHUNKS = 2
PER = 8 // CHUNKS
AREA = NY * NZH * PER
GROUP = 8
SLOTS = 384
VMEM = 60 * 1024 * 1024
BF = jnp.bfloat16
F32 = jnp.float32


def moved(index, count, step):
    return (index + step) % count


def row_perm(dx=0, dzl=0):
    return [
        (x * NZL + z, moved(x, NX, dx) * NZL + moved(z, NZL, dzl))
        for x in range(NX)
        for z in range(NZL)
    ]


def col_perm(dy=0, dzh=0, dco=0):
    return [
        (
            (y * NZH + z) * NCO + c,
            (moved(y, NY, dy) * NZH + moved(z, NZH, dzh)) * NCO + moved(c, NCO, dco),
        )
        for y in range(NY)
        for z in range(NZH)
        for c in range(NCO)
    ]


def send_row(value, **step):
    return lax.ppermute(value, "row", row_perm(**step))


def send_col(value, **step):
    return lax.ppermute(value, "col", col_perm(**step))


def in_smem():
    return pl.BlockSpec(memory_space=pltpu.SMEM)


def in_vmem():
    return pl.BlockSpec(memory_space=pltpu.VMEM)


def in_any():
    return pl.BlockSpec(memory_space=pl.ANY)


def shape_of(rows, dtype):
    return jax.ShapeDtypeStruct((rows, EDGE), dtype)


def params():
    return pltpu.CompilerParams(vmem_limit_bytes=VMEM)


def bins_kernel(slots, place_ref, count_ref, rows_ref, cols_ref, list_ref, number_ref):
    row, col = place_ref[0], place_ref[1]
    my_x, my_zl = row >> 1, row & 1
    my_y, my_zh, my_co = col >> 3, (col >> 1) & 3, col & 1
    parts = 2 * CHUNKS
    for part in range(parts):
        number_ref[part] = 0

    def one(slot, carry):
        tile = rows_ref[slot]
        owner, inner = tile >> 3, tile & 7
        dy = ((owner >> 3) - my_y) & 3
        dz = (((owner >> 1) & 3) - my_zh) & 3
        part = (inner // PER) * 2 + ((owner & 1) ^ my_co)
        row_place = (dy * NZH + dz) * PER + inner % PER
        tile = cols_ref[slot]
        owner, inner = tile >> 3, tile & 7
        dx = ((owner >> 1) - my_x) & 3
        col_place = (dx * 2 + ((owner & 1) ^ my_zl)) * 8 + inner
        at = number_ref[part]
        list_ref[part * SLOTS + at] = slot | (col_place << 9) | (row_place << 16)
        number_ref[part] = at + 1
        return carry

    lax.fori_loop(0, count_ref[0], one, 0)
    for part in range(parts):
        last = number_ref[part]
        for extra in range(GROUP - 1):
            list_ref[part * SLOTS + last + extra] = 64 << 9


def make_bins(place, count, slot_rows, slot_cols):
    return pl.pallas_call(
        functools.partial(bins_kernel, slot_rows.shape[0]),
        out_shape=(
            jax.ShapeDtypeStruct((2 * CHUNKS * SLOTS,), jnp.int32),
            jax.ShapeDtypeStruct((2 * CHUNKS,), jnp.int32),
        ),
        in_specs=[in_smem()] * 4,
        out_specs=(in_smem(), in_smem()),
        compiler_params=params(),
        name="bins",
    )(place, count, slot_rows, slot_cols)


def groups_of(number_ref, part):
    return (number_ref[part] + (GROUP - 1)) // GROUP


def start_tiles(list_ref, tiles_ref, buffer, sems, part, groups, first_group):
    def issue(group, carry):
        for k in range(GROUP):
            entry = list_ref[part * SLOTS + group * GROUP + k]
            pltpu.make_async_copy(
                tiles_ref.at[entry & 511],
                buffer.at[(first_group + group) * GROUP + k],
                sems.at[first_group + group],
            ).start()
        return carry

    lax.fori_loop(0, groups, issue, 0)


def wait_group(tiles_ref, buffer, sems, group):
    pltpu.make_async_copy(
        tiles_ref.at[pl.ds(0, GROUP)],
        buffer.at[pl.ds(group * GROUP, GROUP)],
        sems.at[group],
    ).wait()


def place(index):
    return pl.ds(pl.multiple_of(index * EDGE, EDGE), EDGE)


BATCH = 4


def forward_sum(part, list_ref, number_ref, pieces, tiles_ref, xbuf, tbuf, acc, xsem, tsem, start):
    groups = groups_of(number_ref, part)
    copies = [
        pltpu.make_async_copy(piece, xbuf.at[pl.ds(k * 1024, 1024)], xsem.at[k])
        for k, piece in enumerate(pieces)
    ]
    for copy in copies:
        copy.start()
    start_tiles(list_ref, tiles_ref, tbuf, tsem, part, groups, 0)
    start()
    xbuf[pl.ds(64 * EDGE, EDGE), :] = jnp.zeros((EDGE, EDGE), BF)
    for copy in copies:
        copy.wait()

    def body(group, carry):
        wait_group(tiles_ref, tbuf, tsem, group)
        for first in range(0, GROUP, BATCH):
            entries = [
                list_ref[part * SLOTS + group * GROUP + first + k] for k in range(BATCH)
            ]
            products = [
                jnp.dot(
                    tbuf[group * GROUP + first + k],
                    xbuf[place((entry >> 9) & 127), :],
                    preferred_element_type=F32,
                )
                for k, entry in enumerate(entries)
            ]
            for entry, product in zip(entries, products):
                acc[place(entry >> 16), :] += product
        return carry

    lax.fori_loop(0, groups, body, 0)


def over_tiles(count, step):
    def one(index, carry):
        step(place(index))
        return carry

    lax.fori_loop(0, count, one, 0)


def forward_send_kernel(part, list_ref, number_ref, *refs):
    pieces, (tiles_ref, out_ref, xbuf, tbuf, acc, xsem, tsem) = refs[:8], refs[8:]

    def start():
        def clear(at):
            acc[at, :] = jnp.zeros((EDGE, EDGE), F32)

        over_tiles(AREA, clear)

    forward_sum(part, list_ref, number_ref, pieces, tiles_ref, xbuf, tbuf, acc, xsem, tsem, start)

    def store(at):
        out_ref[at, :] = acc[at, :].astype(BF)

    over_tiles(AREA, store)


def forward_keep_kernel(part, list_ref, number_ref, *refs):
    pieces, refs = refs[:8], refs[8:]
    tiles_ref, got_ref, to_right, to_left, rest_right, rest_left, own, xbuf, tbuf, acc, xsem, tsem = refs

    def start():
        def load(at):
            acc[at, :] = got_ref[at, :].astype(F32)

        over_tiles(AREA, load)

    forward_sum(part, list_ref, number_ref, pieces, tiles_ref, xbuf, tbuf, acc, xsem, tsem, start)
    split_ring(acc, AREA * EDGE // 4, to_right, to_left, rest_right, rest_left, own)


def split_ring(acc, block, to_right, to_left, rest_right, rest_left, own):
    half = block // 2
    rows = 128
    for k in range(0, half, rows):
        at, low = pl.ds(k, rows), pl.ds(half + k, rows)
        to_right[at, :] = acc[pl.ds(2 * block + k, rows), :].astype(BF)
        to_right[low, :] = acc[pl.ds(block + half + k, rows), :].astype(BF)
        to_left[at, :] = acc[pl.ds(2 * block + half + k, rows), :].astype(BF)
        to_left[low, :] = acc[pl.ds(3 * block + k, rows), :].astype(BF)
        rest_right[at, :] = acc[pl.ds(block + k, rows), :]
        rest_left[at, :] = acc[pl.ds(3 * block + half + k, rows), :]
        own[at, :] = acc[at, :]
        own[low, :] = acc[low, :]


def ring_shapes(block):
    half = block // 2
    return (
        shape_of(block, BF),
        shape_of(block, BF),
        shape_of(half, F32),
        shape_of(half, F32),
        shape_of(block, F32),
    )


def forward_scratch():
    return [
        pltpu.VMEM((65 * EDGE, EDGE), BF),
        pltpu.VMEM((SLOTS, EDGE, EDGE), BF),
        pltpu.VMEM((AREA * EDGE, EDGE), F32),
        pltpu.SemaphoreType.DMA((8,)),
        pltpu.SemaphoreType.DMA((SLOTS // GROUP,)),
    ]


def forward_send(part, lists, numbers, pieces, tiles):
    return pl.pallas_call(
        functools.partial(forward_send_kernel, part),
        out_shape=shape_of(AREA * EDGE, BF),
        in_specs=[in_smem()] * 2 + [in_any()] * 9,
        out_specs=in_vmem(),
        scratch_shapes=forward_scratch(),
        compiler_params=params(),
        name="forward_send",
    )(lists, numbers, *pieces, tiles)


def forward_keep(part, lists, numbers, pieces, tiles, got):
    return pl.pallas_call(
        functools.partial(forward_keep_kernel, part),
        out_shape=ring_shapes(AREA * EDGE // 4),
        in_specs=[in_smem()] * 2 + [in_any()] * 9 + [in_vmem()],
        out_specs=(in_vmem(),) * 5,
        scratch_shapes=forward_scratch(),
        compiler_params=params(),
        name="forward_keep",
    )(lists, numbers, *pieces, tiles, got)


def ring_middle(rest_right, rest_left, from_left, from_right):
    half = rest_right.shape[0]
    on_right = (rest_right + from_left[:half].astype(F32)).astype(BF)
    on_left = (rest_left + from_right[:half].astype(F32)).astype(BF)
    return on_right, on_left


def ring_total(own, from_left, from_right, late_left, late_right):
    half = late_left.shape[0]
    first = own[:half] + from_right[half:].astype(F32) + late_left.astype(F32)
    second = own[half:] + from_left[half:].astype(F32) + late_right.astype(F32)
    return first, second


def turn_kernel(own, from_left, from_right, late_left, late_right, to_right, to_left, rest_right, rest_left, mine, acc):
    half = late_left.shape[0]
    acc[pl.ds(0, half), :] = own[pl.ds(0, half), :] + from_right[pl.ds(half, half), :].astype(F32) + late_left[...].astype(F32)
    acc[pl.ds(half, half), :] = own[pl.ds(half, half), :] + from_left[pl.ds(half, half), :].astype(F32) + late_right[...].astype(F32)
    split_ring(acc, own.shape[0] // 4, to_right, to_left, rest_right, rest_left, mine)


def ring_turn(own, from_left, from_right, late_left, late_right):
    return pl.pallas_call(
        turn_kernel,
        out_shape=ring_shapes(own.shape[0] // 4),
        in_specs=[in_vmem()] * 5,
        out_specs=(in_vmem(),) * 5,
        scratch_shapes=[pltpu.VMEM(own.shape, F32)],
        compiler_params=params(),
        name="turn",
    )(own, from_left, from_right, late_left, late_right)


def dense_kernel(chunk, own, from_left, from_right, late_left, late_right, weight_ref, bias_ref, cot_ref, *refs):
    if chunk:
        act_in, terms_in, act_ref, back_ref, terms_ref = refs
    else:
        act_ref, back_ref, terms_ref = refs
    half = late_left.shape[0]
    rows = 2 * half
    first = own[pl.ds(0, half), :] + from_right[pl.ds(half, half), :].astype(F32) + late_left[...].astype(F32)
    second = own[pl.ds(half, half), :] + from_left[pl.ds(half, half), :].astype(F32) + late_right[...].astype(F32)
    hidden = jnp.concatenate([first.astype(BF), second.astype(BF)], axis=0)
    weight = weight_ref[...]
    pre = jnp.dot(hidden, weight, preferred_element_type=F32) + bias_ref[...]
    sigma = jax.nn.sigmoid(pre)
    act = (pre * sigma).astype(BF)
    cot = cot_ref[pl.ds(chunk * rows, rows), :].astype(F32)
    grad_pre = cot * sigma * (1.0 + pre * (1.0 - sigma))
    grad_round = grad_pre.astype(BF)
    weight_term = lax.dot_general(hidden, grad_round, (((0,), (0,)), ((), ())), preferred_element_type=F32)
    bias_term = jnp.broadcast_to(jnp.sum(grad_pre, axis=0, keepdims=True), (8, EDGE))
    for tile in range(rows // EDGE):
        part = grad_round[tile * EDGE : (tile + 1) * EDGE, :]
        back = lax.dot_general(weight, part, (((1,), (1,)), ((), ())), preferred_element_type=F32)
        back_ref[pl.ds(tile * EDGE, EDGE), :] = back.astype(BF)
    if chunk:
        act_ref[pl.ds(0, rows), :] = act_in[...]
        act_ref[pl.ds(rows, rows), :] = act
        terms_ref[pl.ds(0, EDGE), :] = terms_in[pl.ds(0, EDGE), :] + weight_term
        terms_ref[pl.ds(EDGE, 8), :] = terms_in[pl.ds(EDGE, 8), :] + bias_term
    else:
        act_ref[...] = act
        terms_ref[pl.ds(0, EDGE), :] = weight_term
        terms_ref[pl.ds(EDGE, 8), :] = bias_term


def dense(chunk, own, from_left, from_right, late_left, late_right, weight, bias, cotangent, before):
    rows = own.shape[0]
    return pl.pallas_call(
        functools.partial(dense_kernel, chunk),
        out_shape=(shape_of(rows * (chunk + 1), BF), shape_of(rows, BF), shape_of(EDGE + 8, F32)),
        in_specs=[in_vmem()] * (8 + len(before)),
        out_specs=(in_vmem(),) * 3,
        compiler_params=params(),
        name="dense",
    )(own, from_left, from_right, late_left, late_right, weight, bias, cotangent, *before)


def backward_kernel(chunk, sizes, list_ref, number_ref, *refs):
    count = len(sizes)
    sources, refs = refs[:count], refs[count:]
    tiles_ref, refs = refs[0], refs[1:]
    if chunk:
        before_ref, to_right, to_left, rest_right, rest_left, own, gbuf, tbuf, acc, gsem, tsem, bsem = refs
    else:
        out_ref, gbuf, tbuf, acc, gsem, tsem = refs
    parts = (2 * chunk, 2 * chunk + 1)
    groups = [groups_of(number_ref, part) for part in parts]
    copies, at = [], 0
    for k, size in enumerate(sizes):
        copies.append(pltpu.make_async_copy(sources[k], gbuf.at[pl.ds(at, size)], gsem.at[k]))
        at += size
    for copy in copies:
        copy.start()
    if chunk:
        whole = pltpu.make_async_copy(before_ref, acc.at[pl.ds(0, 64 * EDGE)], bsem.at[0])
        whole.start()
    start_tiles(list_ref, tiles_ref, tbuf, tsem, parts[0], groups[0], 0)
    start_tiles(list_ref, tiles_ref, tbuf, tsem, parts[1], groups[1], groups[0])
    if chunk:
        whole.wait()
        acc[pl.ds(64 * EDGE, EDGE), :] = jnp.zeros((EDGE, EDGE), F32)
    else:

        def clear(at):
            acc[at, :] = jnp.zeros((EDGE, EDGE), F32)

        over_tiles(65, clear)
    for copy in copies:
        copy.wait()
    for which, part in enumerate(parts):
        first_group = groups[0] * which

        def body(group, carry):
            wait_group(tiles_ref, tbuf, tsem, first_group + group)
            for first in range(0, GROUP, BATCH):
                entries = [
                    list_ref[part * SLOTS + group * GROUP + first + k] for k in range(BATCH)
                ]
                products = [
                    jnp.dot(
                        gbuf[place(which * AREA + (entry >> 16)), :],
                        tbuf[(first_group + group) * GROUP + first + k],
                        preferred_element_type=F32,
                    )
                    for k, entry in enumerate(entries)
                ]
                for entry, product in zip(entries, products):
                    acc[place((entry >> 9) & 127), :] += product
            return carry

        lax.fori_loop(0, groups[which], body, 0)
    if chunk:
        split_ring(acc, 16 * EDGE, to_right, to_left, rest_right, rest_left, own)
    else:

        def store(at):
            out_ref[at, :] = acc[at, :]

        over_tiles(64, store)


def backward(chunk, lists, numbers, sources, tiles, before):
    sizes = tuple(source.shape[0] for source in sources)
    scratch = [
        pltpu.VMEM((2 * AREA * EDGE, EDGE), BF),
        pltpu.VMEM((SLOTS + GROUP, EDGE, EDGE), BF),
        pltpu.VMEM((65 * EDGE, EDGE), F32),
        pltpu.SemaphoreType.DMA((len(sizes),)),
        pltpu.SemaphoreType.DMA((SLOTS // GROUP + 1,)),
    ]
    if chunk:
        scratch.append(pltpu.SemaphoreType.DMA((1,)))
    return pl.pallas_call(
        functools.partial(backward_kernel, chunk, sizes),
        out_shape=ring_shapes(16 * EDGE) if chunk else shape_of(64 * EDGE, F32),
        in_specs=[in_smem()] * 2 + [in_any()] * (len(sizes) + 1 + len(before)),
        out_specs=(in_vmem(),) * 5 if chunk else in_vmem(),
        scratch_shapes=scratch,
        compiler_params=params(),
        name="backward",
    )(lists, numbers, *sources, tiles, *before)


def last_kernel(mine_ref, got_ref, out_ref):
    total = mine_ref[...] + got_ref[...].astype(F32)
    for tile in range(8):
        out_ref[pl.ds(tile * EDGE, EDGE), :] = total[tile * EDGE : (tile + 1) * EDGE, :].T.astype(BF)


def last(mine, got):
    return pl.pallas_call(
        last_kernel,
        out_shape=shape_of(mine.shape[0], BF),
        in_specs=[in_vmem()] * 2,
        out_specs=in_vmem(),
        compiler_params=params(),
        name="last",
    )(mine, got)


def sum_everywhere(terms):
    def swap(value, axis, perm):
        return value + lax.ppermute(value, axis, perm)

    def ring_pairs(size, inner, first):
        other = {0: 1, 1: 0, 2: 3, 3: 2} if first else {0: 3, 3: 0, 1: 2, 2: 1}
        return lambda a: other[a]

    near, far = {0: 1, 1: 0, 2: 3, 3: 2}, {0: 3, 3: 0, 1: 2, 2: 1}
    terms = swap(terms, "col", col_perm(dco=1))
    for pairs in (near, far):
        perm = [((y * 4 + z) * 2 + c, (pairs[y] * 4 + z) * 2 + c) for y in range(4) for z in range(4) for c in range(2)]
        terms = swap(terms, "col", perm)
    for pairs in (near, far):
        perm = [((y * 4 + z) * 2 + c, (y * 4 + pairs[z]) * 2 + c) for y in range(4) for z in range(4) for c in range(2)]
        terms = swap(terms, "col", perm)
    terms = swap(terms, "row", row_perm(dzl=1))
    for pairs in (near, far):
        perm = [(x * 2 + z, pairs[x] * 2 + z) for x in range(4) for z in range(2)]
        terms = swap(terms, "row", perm)
    return terms


def on_device(features, tiles, tile_rows, tile_cols, tile_count, weight, bias, cotangent):
    tile_set = tiles[0, 0]
    spot = jnp.stack([lax.axis_index("row"), lax.axis_index("col")]).astype(jnp.int32)
    lists, numbers = make_bins(spot, tile_count[0], tile_rows[0, 0], tile_cols[0, 0])

    mine = features
    beside = send_row(mine, dzl=1)
    mine_left, mine_right = send_row(mine, dx=1), send_row(mine, dx=-1)
    beside_left, beside_right = send_row(beside, dx=1), send_row(beside, dx=-1)
    mine_far = send_row(mine_left, dx=1)
    beside_far = send_row(beside_right, dx=-1)
    pieces = (mine, beside, mine_right, beside_right, mine_far, beside_far, mine_left, beside_left)

    sent = [forward_send(2 * c + 1, lists, numbers, pieces, tile_set) for c in range(CHUNKS)]
    got = [send_col(s, dco=1) for s in sent]
    bias_row = bias.reshape(1, EDGE)
    before, carried = (), ()
    for c in range(CHUNKS):
        to_right, to_left, rest_right, rest_left, own = forward_keep(2 * c, lists, numbers, pieces, tile_set, got[c])
        from_left, from_right = send_col(to_right, dy=1), send_col(to_left, dy=-1)
        on_right, on_left = ring_middle(rest_right, rest_left, from_left, from_right)
        late_left, late_right = send_col(on_right, dy=1), send_col(on_left, dy=-1)
        to_right, to_left, rest_right, rest_left, own = ring_turn(own, from_left, from_right, late_left, late_right)
        from_left, from_right = send_col(to_right, dzh=1), send_col(to_left, dzh=-1)
        on_right, on_left = ring_middle(rest_right, rest_left, from_left, from_right)
        late_left, late_right = send_col(on_right, dzh=1), send_col(on_left, dzh=-1)
        act, back, terms = dense(
            c, own, from_left, from_right, late_left, late_right, weight, bias_row, cotangent, before
        )
        before = (act, terms)

        half = back.shape[0] // 2
        z_left, z_right = send_col(back, dzh=1), send_col(back, dzh=-1)
        far_a, far_b = send_col(z_left[:half], dzh=1), send_col(z_right[half:], dzh=-1)
        low = jnp.concatenate([back, z_right])
        high = jnp.concatenate([far_a, far_b, z_left])
        low_left, low_right = send_col(low, dy=1), send_col(low, dy=-1)
        high_left, high_right = send_col(high, dy=1), send_col(high, dy=-1)
        low_far = send_col(low_left, dy=1)
        high_far = send_col(high_right, dy=-1)
        near = jnp.concatenate([low, high, low_right, high_right, low_left, high_left])
        far = jnp.concatenate([low_far, high_far])
        near_other, far_other = send_col(near, dco=1), send_col(far, dco=1)
        cut = low.shape[0] * 4
        sources = (low, high, low_right, high_right, low_far, high_far, low_left, high_left)
        others = (near_other[:cut], far_other, near_other[cut:])
        carried = backward(c, lists, numbers, sources + others, tile_set, (carried,) if c else ())

    to_right, to_left, rest_right, rest_left, own = carried
    from_left, from_right = send_row(to_right, dx=1), send_row(to_left, dx=-1)
    on_right, on_left = ring_middle(rest_right, rest_left, from_left, from_right)
    late_left, late_right = send_row(on_right, dx=1), send_row(on_left, dx=-1)
    mine, other = ring_total(own, from_left, from_right, late_left, late_right)
    grad_features = last(mine, send_row(other.astype(BF), dzl=1))

    terms = sum_everywhere(before[1])
    return act, grad_features, terms[:EDGE], terms[EDGE]


def solution(mesh):
    placed = (
        P(("row", "col"), None),
        P("row", "col", None, None, None),
        P("row", "col", None),
        P("row", "col", None),
        P("row", "col"),
        P(),
        P(),
        P(("row", "col"), None),
    )
    return jax.shard_map(
        on_device,
        mesh=mesh,
        in_specs=placed,
        out_specs=(P(("row", "col"), None), P(("row", "col"), None), P(), P()),
        check_vma=False,
    )
```

```python
import functools

import jax
import jax.numpy as jnp
from jax import lax
from jax.experimental import pallas as pl
from jax.experimental.pallas import tpu as pltpu
from jax.sharding import PartitionSpec as P

NX, NZL, NY, NZH, NCO = 4, 2, 4, 4, 2
EDGE = 128
PARTS = (4, 4)
AREAS = tuple(NY * NZH * tiles for tiles in PARTS)
TERMS = EDGE + 16
BLOCK0 = PARTS[0] * EDGE + TERMS
BLOCK1 = PARTS[1] * EDGE + TERMS + 16
SENT = 8 * EDGE + TERMS
GROUP = 8
SLOTS = 384
VMEM = 64 * 1024 * 1024 - 64 * 1024
BF = jnp.bfloat16
F32 = jnp.float32


def moved(index, count, step):
    return (index + step) % count


def row_perm(dx=0, dzl=0):
    return [
        (x * NZL + z, moved(x, NX, dx) * NZL + moved(z, NZL, dzl))
        for x in range(NX)
        for z in range(NZL)
    ]


def col_perm(dy=0, dzh=0, dco=0):
    return [
        (
            (y * NZH + z) * NCO + c,
            (moved(y, NY, dy) * NZH + moved(z, NZH, dzh)) * NCO + moved(c, NCO, dco),
        )
        for y in range(NY)
        for z in range(NZH)
        for c in range(NCO)
    ]


def send_row(value, **step):
    return lax.ppermute(value, "row", row_perm(**step))


def send_col(value, **step):
    return lax.ppermute(value, "col", col_perm(**step))


def in_smem():
    return pl.BlockSpec(memory_space=pltpu.SMEM)


def in_vmem():
    return pl.BlockSpec(memory_space=pltpu.VMEM)


def in_any():
    return pl.BlockSpec(memory_space=pl.ANY)


def shape_of(rows, dtype):
    return jax.ShapeDtypeStruct((rows, EDGE), dtype)


def params():
    return pltpu.CompilerParams(vmem_limit_bytes=VMEM)


def slot_entries(row_tiles, col_tiles):
    row, col = lax.axis_index("row"), lax.axis_index("col")
    my_x, my_zl = row >> 1, row & 1
    my_y, my_zh, my_co = col >> 3, (col >> 1) & 3, col & 1
    owner, inner = row_tiles >> 3, row_tiles & 7
    dy = ((owner >> 3) - my_y) & 3
    dz = (((owner >> 1) & 3) - my_zh) & 3
    other = (owner & 1) ^ my_co
    later = inner >= PARTS[0]
    part = later.astype(jnp.int32) * 2 + other
    ring = dy * NZH + dz
    row_place = jnp.where(later, ring * PARTS[1] + inner - PARTS[0], ring * PARTS[0] + inner)
    source = jnp.where(
        later,
        (NY * NZH * NCO * BLOCK0 + TERMS + 16) // 16
        + (other * NY * NZH + ring) * (BLOCK1 // 16)
        + (inner - PARTS[0]) * (EDGE // 16),
        owner * (BLOCK0 // 16) + inner * (EDGE // 16),
    )
    backward = col_tiles | (source << 7)
    owner, inner = col_tiles >> 3, col_tiles & 7
    dx = ((owner >> 1) - my_x) & 3
    col_place = (dx * 2 + ((owner & 1) ^ my_zl)) * 8 + inner
    slot = lax.broadcasted_iota(jnp.int32, row_tiles.shape, row_tiles.ndim - 1)
    return part, slot | (col_place << 9) | (row_place << 16), backward


def bins_kernel(count_ref, part_ref, entry_ref, list_ref, number_ref):
    for part in range(4):
        number_ref[part] = 0

    def one(slot, carry):
        part = part_ref[slot]
        at = number_ref[part]
        list_ref[part * SLOTS + at] = entry_ref[slot]
        number_ref[part] = at + 1
        return carry

    count = count_ref[0, 0]
    number_ref[4] = count
    lax.fori_loop(0, count, one, 0)
    for part in range(4):
        last = number_ref[part]
        for extra in range(GROUP - 1):
            list_ref[part * SLOTS + last + extra] = 64 << 9


def make_bins(count, part, entry):
    return pl.pallas_call(
        bins_kernel,
        out_shape=(
            jax.ShapeDtypeStruct((4 * SLOTS,), jnp.int32),
            jax.ShapeDtypeStruct((8,), jnp.int32),
        ),
        in_specs=[in_smem()] * 3,
        out_specs=(in_smem(),) * 2,
        compiler_params=params(),
        name="bins",
    )(count, part, entry)


def groups_of(number_ref, part):
    return (number_ref[part] + (GROUP - 1)) // GROUP


def start_tiles(list_ref, tiles_ref, buffer, sems, part, groups, first_group):
    def issue(group, carry):
        for k in range(GROUP):
            entry = list_ref[part * SLOTS + group * GROUP + k]
            pltpu.make_async_copy(
                tiles_ref.at[entry & 511],
                buffer.at[(first_group + group) * GROUP + k],
                sems.at[first_group + group],
            ).start()
        return carry

    lax.fori_loop(0, groups, issue, 0)


def wait_group(tiles_ref, buffer, sems, group):
    pltpu.make_async_copy(
        tiles_ref.at[pl.ds(0, GROUP)],
        buffer.at[pl.ds(group * GROUP, GROUP)],
        sems.at[group],
    ).wait()


def place(index):
    return pl.ds(pl.multiple_of(index * EDGE, EDGE), EDGE)


BATCH = 4


def forward_sum(part, list_ref, number_ref, pieces, tiles_ref, xbuf, tbuf, acc, xsem, tsem, start):
    groups = groups_of(number_ref, part)
    copies = [
        pltpu.make_async_copy(piece, xbuf.at[pl.ds(k * 1024, 1024)], xsem.at[k])
        for k, piece in enumerate(pieces)
    ]
    for copy in copies:
        copy.start()
    start_tiles(list_ref, tiles_ref, tbuf, tsem, part, groups, 0)
    start()
    xbuf[pl.ds(64 * EDGE, EDGE), :] = jnp.zeros((EDGE, EDGE), BF)
    for copy in copies:
        copy.wait()

    def body(group, carry):
        wait_group(tiles_ref, tbuf, tsem, group)
        for first in range(0, GROUP, BATCH):
            entries = [
                list_ref[part * SLOTS + group * GROUP + first + k] for k in range(BATCH)
            ]
            products = [
                jnp.dot(
                    tbuf[group * GROUP + first + k],
                    xbuf[place((entry >> 9) & 127), :],
                    preferred_element_type=F32,
                )
                for k, entry in enumerate(entries)
            ]
            for entry, product in zip(entries, products):
                acc[place(entry >> 16), :] += product
        return carry

    lax.fori_loop(0, groups, body, 0)


def over_tiles(count, step):
    def one(index, carry):
        step(place(index))
        return carry

    lax.fori_loop(0, count, one, 0)


def forward_send_kernel(part, list_ref, number_ref, *refs):
    pieces, (tiles_ref, out_ref, xbuf, tbuf, acc, xsem, tsem) = refs[:8], refs[8:]

    def start():
        def clear(at):
            acc[at, :] = jnp.zeros((EDGE, EDGE), F32)

        over_tiles(AREAS[part], clear)

    forward_sum(2 * part + 1, list_ref, number_ref, pieces, tiles_ref, xbuf, tbuf, acc, xsem, tsem, start)

    def store(at):
        out_ref[at, :] = acc[at, :].astype(BF)

    over_tiles(AREAS[part], store)


def forward_keep_kernel(part, list_ref, number_ref, *refs):
    pieces, refs = refs[:8], refs[8:]
    tiles_ref, got_ref, own, to_right, to_left, rest_right, rest_left, xbuf, tbuf, acc, xsem, tsem = refs

    def start():
        def load(at):
            acc[at, :] = got_ref[at, :].astype(F32)

        over_tiles(AREAS[part], load)

    forward_sum(2 * part, list_ref, number_ref, pieces, tiles_ref, xbuf, tbuf, acc, xsem, tsem, start)
    split_relay(lambda k, rows: acc[pl.ds(k, rows), :], own, to_right, to_left, rest_right, rest_left)


def split_relay(read, own, to_right, to_left, rest_right, rest_left):
    block = own.shape[0]
    half = block // 2
    for k in range(0, half, 64):
        at, low = pl.ds(k, 64), pl.ds(half + k, 64)
        own[at, :] = read(k, 64)
        own[low, :] = read(half + k, 64)
        to_right[at, :] = read(2 * block + k, 64).astype(BF)
        to_right[low, :] = read(block + half + k, 64).astype(BF)
        to_left[at, :] = read(2 * block + half + k, 64).astype(BF)
        to_left[low, :] = read(3 * block + k, 64).astype(BF)
        rest_right[at, :] = read(block + k, 64)
        rest_left[at, :] = read(3 * block + half + k, 64)


def relay_shapes(block):
    half = block // 2
    return (shape_of(block, F32),) + (shape_of(block, BF),) * 2 + (shape_of(half, F32),) * 2


def forward_scratch(part):
    return [
        pltpu.VMEM((65 * EDGE, EDGE), BF),
        pltpu.VMEM((SLOTS, EDGE, EDGE), BF),
        pltpu.VMEM((AREAS[part] * EDGE, EDGE), F32),
        pltpu.SemaphoreType.DMA((8,)),
        pltpu.SemaphoreType.DMA((SLOTS // GROUP,)),
    ]


def forward_send(part, lists, numbers, pieces, tiles):
    return pl.pallas_call(
        functools.partial(forward_send_kernel, part),
        out_shape=shape_of(AREAS[part] * EDGE, BF),
        in_specs=[in_smem()] * 2 + [in_any()] * 9,
        out_specs=in_vmem(),
        scratch_shapes=forward_scratch(part),
        compiler_params=params(),
        name="forward_send",
    )(lists, numbers, *pieces, tiles)


def forward_keep(part, lists, numbers, pieces, tiles, got):
    return pl.pallas_call(
        functools.partial(forward_keep_kernel, part),
        out_shape=relay_shapes(AREAS[part] * EDGE // 4),
        in_specs=[in_smem()] * 2 + [in_any()] * 9 + [in_vmem()],
        out_specs=(in_vmem(),) * 5,
        scratch_shapes=forward_scratch(part),
        compiler_params=params(),
        name="forward_keep",
    )(lists, numbers, *pieces, tiles, got)


def relay_total(own, from_left, from_right, late_left, late_right):
    half = late_left.shape[0]

    def read(k, rows):
        at = pl.ds(k, rows)
        if k < half:
            return own[at, :] + from_right[pl.ds(half + k, rows), :].astype(F32) + late_left[at, :].astype(F32)
        return own[at, :] + from_left[at, :].astype(F32) + late_right[pl.ds(k - half, rows), :].astype(F32)

    return read


def middle_kernel(rest_right, rest_left, from_left, from_right, on_right, on_left):
    half = rest_right.shape[0]
    on_right[...] = (rest_right[...] + from_left[pl.ds(0, half), :].astype(F32)).astype(BF)
    on_left[...] = (rest_left[...] + from_right[pl.ds(0, half), :].astype(F32)).astype(BF)


def relay_middle(rest_right, rest_left, from_left, from_right):
    return pl.pallas_call(
        middle_kernel,
        out_shape=(shape_of(rest_right.shape[0], BF),) * 2,
        in_specs=[in_vmem()] * 4,
        out_specs=(in_vmem(),) * 2,
        compiler_params=params(),
        name="middle",
    )(rest_right, rest_left, from_left, from_right)


def turn_kernel(*refs):
    split_relay(relay_total(*refs[:5]), *refs[5:])


def ring_turn(*values):
    return pl.pallas_call(
        turn_kernel,
        out_shape=relay_shapes(values[0].shape[0] // 4),
        in_specs=[in_vmem()] * 5,
        out_specs=(in_vmem(),) * 5,
        compiler_params=params(),
        name="turn",
    )(*values)


def join_kernel(count, *refs):
    pieces, out_ref = refs[:count], refs[count]
    at = 0
    for piece in pieces:
        out_ref[pl.ds(at, piece.shape[0]), :] = piece[...]
        at += piece.shape[0]


def join(pieces):
    return pl.pallas_call(
        functools.partial(join_kernel, len(pieces)),
        out_shape=shape_of(sum(p.shape[0] for p in pieces), BF),
        in_specs=[in_vmem()] * len(pieces),
        out_specs=in_vmem(),
        compiler_params=params(),
        name="join",
    )(*pieces)


def dense_kernel(chunk, *refs):
    sums, (weight_ref, bias_ref, cot_ref), outs = refs[:5], refs[5:8], refs[8:]
    rows = PARTS[chunk] * EDGE
    skip = chunk * PARTS[0] * EDGE
    read = relay_total(*sums)
    hidden = jnp.concatenate([read(k, rows // 2).astype(BF) for k in (0, rows // 2)], axis=0)
    weight = weight_ref[...]
    pre = jnp.dot(hidden, weight, preferred_element_type=F32) + bias_ref[...]
    sigma = jax.nn.sigmoid(pre)
    act = (pre * sigma).astype(BF)
    if chunk:
        act_in, (act_ref, block_ref) = outs[0], outs[1:]
        act_ref[pl.ds(0, skip), :] = act_in[...]
        act_ref[pl.ds(skip, rows), :] = act
        terms_at, back_at = 0, TERMS + 16
        block_ref[pl.ds(TERMS, 16), :] = jnp.zeros((16, EDGE), BF)
    else:
        act_ref, block_ref = outs
        act_ref[...] = act
        terms_at, back_at = rows, 0
    grad_pre = cot_ref[pl.ds(skip, rows), :].astype(F32) * sigma * (1.0 + pre * (1.0 - sigma))
    grad_round = grad_pre.astype(BF)
    weight_term = lax.dot_general(hidden, grad_round, (((0,), (0,)), ((), ())), preferred_element_type=F32)
    bias_term = jnp.broadcast_to(jnp.sum(grad_pre, axis=0, keepdims=True), (16, EDGE))
    block_ref[pl.ds(terms_at, EDGE), :] = weight_term.astype(BF)
    block_ref[pl.ds(terms_at + EDGE, 16), :] = bias_term.astype(BF)
    for tile in range(PARTS[chunk]):
        part = grad_round[tile * EDGE : (tile + 1) * EDGE, :]
        back = lax.dot_general(weight, part, (((1,), (1,)), ((), ())), preferred_element_type=F32)
        block_ref[pl.ds(back_at + tile * EDGE, EDGE), :] = back.astype(BF)


def dense(chunk, sums, weight, bias, cotangent, before):
    return pl.pallas_call(
        functools.partial(dense_kernel, chunk),
        out_shape=(
            shape_of(sum(PARTS[: chunk + 1]) * EDGE, BF),
            shape_of((BLOCK0, BLOCK1)[chunk], BF),
        ),
        in_specs=[in_vmem()] * (8 + len(before)),
        out_specs=(in_vmem(),) * 2,
        compiler_params=params(),
        name="dense",
    )(*sums, weight, bias, cotangent, *before)


def both_ways(values):
    return (values[0] + values[2]) + (values[1] + values[3])


def backward_kernel(sizes, back_ref, number_ref, *refs):
    count = len(sizes)
    sources, tiles_ref = refs[:count], refs[count]
    out_ref, gbuf, tbuf, acc, gsem, tsem = refs[count + 1 :]
    groups = (number_ref[4] + (GROUP - 1)) // GROUP
    slots = tiles_ref.shape[0]
    copies, at = [], 0
    for k, size in enumerate(sizes):
        copies.append(pltpu.make_async_copy(sources[k], gbuf.at[pl.ds(at, size)], gsem.at[k]))
        at += size
    for copy in copies:
        copy.start()

    def tile_copy(group):
        at = pl.ds(group * GROUP, GROUP)
        return pltpu.make_async_copy(tiles_ref.at[at], tbuf.at[at], tsem.at[group])

    def issue(group, carry):
        tile_copy(group).start()
        return carry

    lax.fori_loop(0, groups, issue, 0)

    def clear(at):
        acc[at, :] = jnp.zeros((EDGE, EDGE), F32)

    over_tiles(65, clear)
    for copy in copies:
        copy.wait()

    def entry_of(slot):
        return jnp.where(slot < number_ref[4], back_ref[jnp.minimum(slot, slots - 1)], 64)

    def body(group, carry):
        tile_copy(group).wait()
        for first in range(0, GROUP, BATCH):
            entries = [entry_of(group * GROUP + first + k) for k in range(BATCH)]
            products = [
                jnp.dot(
                    gbuf[pl.ds(pl.multiple_of((entry >> 7) * 16, 16), EDGE), :],
                    tbuf[group * GROUP + first + k],
                    preferred_element_type=F32,
                )
                for k, entry in enumerate(entries)
            ]
            for entry, product in zip(entries, products):
                acc[place(entry & 127), :] += product
        return carry

    lax.fori_loop(0, groups, body, 0)

    second = NY * NZH * NCO * BLOCK0

    def terms_of(k, rows):
        total = jnp.zeros((rows, EDGE), F32)
        for owner in range(NY * NZH * NCO):
            total += gbuf[pl.ds(owner * BLOCK0 + PARTS[0] * EDGE + k, rows), :].astype(F32)
        cores = []
        for core in range(NCO):
            rings = []
            for dy in range(NY):
                first = second + (core * NY + dy) * NZH * BLOCK1 + k
                rings.append(
                    both_ways(
                        [gbuf[pl.ds(first + dz * BLOCK1, rows), :].astype(F32) for dz in range(NZH)]
                    )
                )
            cores.append(both_ways(rings))
        return (total + (cores[0] + cores[1])).astype(BF)

    for k in range(0, TERMS, 48):
        terms = terms_of(k, 48)
        for owner in range(8):
            out_ref[pl.ds(owner * SENT + 8 * EDGE + k, 48), :] = terms
    for owner in range(8):
        for tile in range(8):
            at = pl.ds(owner * SENT + tile * EDGE, EDGE)
            out_ref[at, :] = acc[pl.ds((owner * 8 + tile) * EDGE, EDGE), :].astype(BF)


def backward(backs, numbers, sources, tiles):
    sizes = tuple(source.shape[0] for source in sources)
    return pl.pallas_call(
        functools.partial(backward_kernel, sizes),
        out_shape=shape_of(8 * SENT, BF),
        in_specs=[in_smem()] * 2 + [in_any()] * (len(sizes) + 1),
        out_specs=in_vmem(),
        scratch_shapes=[
            pltpu.VMEM((sum(sizes), EDGE), BF),
            pltpu.VMEM((tiles.shape[0], EDGE, EDGE), BF),
            pltpu.VMEM((65 * EDGE, EDGE), F32),
            pltpu.SemaphoreType.DMA((len(sizes),)),
            pltpu.SemaphoreType.DMA((SLOTS // GROUP,)),
        ],
        compiler_params=params(),
        name="backward",
    )(backs, numbers, *sources, tiles)


def last_kernel(got_ref, out_ref, weight_ref, bias_ref):
    for tile in range(8):
        total = jnp.zeros((EDGE, EDGE), F32)
        for peer in range(8):
            total += got_ref[pl.ds(peer * SENT + tile * EDGE, EDGE), :].astype(F32)
        out_ref[pl.ds(tile * EDGE, EDGE), :] = total.T.astype(BF)
    terms = jnp.zeros((TERMS, EDGE), F32)
    for peer in range(8):
        terms += got_ref[pl.ds(peer * SENT + 8 * EDGE, TERMS), :].astype(F32)
    weight_ref[...] = terms[:EDGE]
    bias_ref[...] = terms[EDGE : EDGE + 1]


def last(got):
    return pl.pallas_call(
        last_kernel,
        out_shape=(shape_of(8 * EDGE, BF), shape_of(EDGE, F32), shape_of(1, F32)),
        in_specs=[in_vmem()],
        out_specs=(in_vmem(),) * 3,
        compiler_params=params(),
        name="last",
    )(got)


def after(value, *others):
    return lax.optimization_barrier((value, *others))[0]


def around(block, axis):
    half = block.shape[0] // 2
    left, right = send_col(block, **{axis: 1}), send_col(block, **{axis: -1})
    return right, send_col(left[:half], **{axis: 1}), send_col(right[half:], **{axis: -1}), left


def on_device(features, tiles, tile_rows, tile_cols, tile_count, weight, bias, cotangent):
    tile_set = tiles[0, 0]
    part, entry, backs = slot_entries(tile_rows[0, 0], tile_cols[0, 0])

    mine = features
    beside = after(send_row(mine, dzl=1), entry)
    mine_left, mine_right = send_row(mine, dx=1), send_row(mine, dx=-1)
    beside_left, beside_right = send_row(beside, dx=1), send_row(beside, dx=-1)
    mine_far = send_row(mine_left, dx=1)
    beside_far = send_row(beside_right, dx=-1)
    pieces = (mine, beside, mine_right, beside_right, mine_far, beside_far, mine_left, beside_left)
    lists, numbers = make_bins(after(tile_count, mine_left, beside_right), part, entry)

    latest = []

    def gate(value):
        return after(value, *latest) if latest else value

    def ran(values):
        latest[:] = [values[0]]
        return values

    both = (0, 1)
    got = []
    for c in both:
        (part,) = ran([forward_send(c, gate(lists), numbers, pieces, tile_set)])
        got.append(send_col(part, dco=1))
    rings = []
    for c in both:
        rings.append(ran(forward_keep(c, gate(lists), numbers, pieces, tile_set, got[c])))
    bias_row = bias.reshape(1, EDGE)
    for axis in ("dy", "dzh"):
        early = [(send_col(r[1], **{axis: 1}), send_col(r[2], **{axis: -1})) for r in rings]
        late = []
        for c in both:
            on_right, on_left = ran(relay_middle(gate(rings[c][3]), rings[c][4], *early[c]))
            late.append((send_col(on_right, **{axis: 1}), send_col(on_left, **{axis: -1})))
        sums = [(rings[c][0],) + early[c] + late[c] for c in both]
        if axis == "dy":
            rings = [ran(ring_turn(gate(own), *others)) for own, *others in sums]
    act, blocks = (), []
    for c in both:
        own, *others = sums[c]
        *act, block = ran(dense(c, (gate(own), *others), weight, bias_row, cotangent, act))
        blocks.append(block)

    gathered = lax.all_gather(blocks[0], "col", axis=0, tiled=True)
    joined = join((blocks[1],) + around(blocks[1], "dzh"))
    sources = (joined,) + around(joined, "dy")
    sources += tuple(send_col(source, dco=1) for source in sources)
    partial = backward(backs, numbers, (gathered,) + sources, tile_set)
    got = lax.all_to_all(partial.reshape(8, SENT, EDGE), "row", 0, 0, tiled=True)
    grad_features, grad_weight, grad_bias = last(got.reshape(8 * SENT, EDGE))
    return act[0], grad_features, grad_weight, grad_bias.reshape(EDGE)


def solution(mesh):
    placed = (
        P(("row", "col"), None),
        P("row", "col", None, None, None),
        P("row", "col", None),
        P("row", "col", None),
        P("row", "col"),
        P(),
        P(),
        P(("row", "col"), None),
    )
    return jax.shard_map(
        on_device,
        mesh=mesh,
        in_specs=placed,
        out_specs=(P(("row", "col"), None), P(("row", "col"), None), P(), P()),
        check_vma=False,
    )
```

```python
import functools

import jax
import jax.numpy as jnp
from jax import lax
from jax.experimental import pallas as pl
from jax.experimental.pallas import tpu as pltpu
from jax.sharding import PartitionSpec as P

NX, NZL, NY, NZH, NCO = 4, 2, 4, 4, 2
EDGE = 128
PARTS = (4, 4)
AREAS = tuple(NY * NZH * tiles for tiles in PARTS)
TERMS = EDGE + 16
BLOCK = PARTS[1] * EDGE + TERMS
SENT = 8 * EDGE + TERMS
GROUP = 8
SLOTS = 384
VMEM = 64 * 1024 * 1024 - 64 * 1024
BF = jnp.bfloat16
F32 = jnp.float32


def moved(index, count, step):
    return (index + step) % count


def row_perm(dx=0, dzl=0):
    return [
        (x * NZL + z, moved(x, NX, dx) * NZL + moved(z, NZL, dzl))
        for x in range(NX)
        for z in range(NZL)
    ]


def col_perm(dy=0, dzh=0, dco=0):
    return [
        (
            (y * NZH + z) * NCO + c,
            (moved(y, NY, dy) * NZH + moved(z, NZH, dzh)) * NCO + moved(c, NCO, dco),
        )
        for y in range(NY)
        for z in range(NZH)
        for c in range(NCO)
    ]


def send_row(value, **step):
    return lax.ppermute(value, "row", row_perm(**step))


def send_col(value, **step):
    return lax.ppermute(value, "col", col_perm(**step))


def in_smem():
    return pl.BlockSpec(memory_space=pltpu.SMEM)


def in_vmem():
    return pl.BlockSpec(memory_space=pltpu.VMEM)


def in_any():
    return pl.BlockSpec(memory_space=pl.ANY)


def shape_of(rows, dtype):
    return jax.ShapeDtypeStruct((rows, EDGE), dtype)


def params():
    return pltpu.CompilerParams(vmem_limit_bytes=VMEM)


def slot_entries(row_tiles, col_tiles):
    row, col = lax.axis_index("row"), lax.axis_index("col")
    my_x, my_zl = row >> 1, row & 1
    my_y, my_zh, my_co = col >> 3, (col >> 1) & 3, col & 1
    owner, inner = row_tiles >> 3, row_tiles & 7
    dy = ((owner >> 3) - my_y) & 3
    dz = (((owner >> 1) & 3) - my_zh) & 3
    other = (owner & 1) ^ my_co
    later = inner >= PARTS[0]
    part = later.astype(jnp.int32) * 2 + other
    ring = dy * NZH + dz
    row_place = jnp.where(later, ring * PARTS[1] + inner - PARTS[0], ring * PARTS[0] + inner)
    source = jnp.where(
        later,
        owner * (BLOCK // 16) + (inner - PARTS[0]) * (EDGE // 16),
        (other * AREAS[0] + row_place) * (EDGE // 16),
    )
    backward = col_tiles | (source << 7)
    owner, inner = col_tiles >> 3, col_tiles & 7
    dx = ((owner >> 1) - my_x) & 3
    col_place = (dx * 2 + ((owner & 1) ^ my_zl)) * 8 + inner
    slot = lax.broadcasted_iota(jnp.int32, row_tiles.shape, row_tiles.ndim - 1)
    return part, slot | (col_place << 9) | (row_place << 16), backward


def bins_kernel(count_ref, part_ref, entry_ref, back_ref, list_ref, backs_ref, number_ref):
    for part in range(4):
        number_ref[part] = 0

    def one(slot, carry):
        part = part_ref[slot]
        at = number_ref[part]
        list_ref[part * SLOTS + at] = entry_ref[slot]
        backs_ref[part * SLOTS + at] = back_ref[slot]
        number_ref[part] = at + 1
        return carry

    lax.fori_loop(0, count_ref[0, 0], one, 0)
    for part in range(4):
        last = number_ref[part]
        for extra in range(GROUP - 1):
            list_ref[part * SLOTS + last + extra] = 64 << 9
            backs_ref[part * SLOTS + last + extra] = 64


def make_bins(count, part, entry, back):
    return pl.pallas_call(
        bins_kernel,
        out_shape=(
            jax.ShapeDtypeStruct((4 * SLOTS,), jnp.int32),
            jax.ShapeDtypeStruct((4 * SLOTS,), jnp.int32),
            jax.ShapeDtypeStruct((4,), jnp.int32),
        ),
        in_specs=[in_smem()] * 4,
        out_specs=(in_smem(),) * 3,
        compiler_params=params(),
        name="bins",
    )(count, part, entry, back)


def groups_of(number_ref, part):
    return (number_ref[part] + (GROUP - 1)) // GROUP


def start_tiles(list_ref, tiles_ref, buffer, sems, part, groups, first_group):
    def issue(group, carry):
        for k in range(GROUP):
            entry = list_ref[part * SLOTS + group * GROUP + k]
            pltpu.make_async_copy(
                tiles_ref.at[entry & 511],
                buffer.at[(first_group + group) * GROUP + k],
                sems.at[first_group + group],
            ).start()
        return carry

    lax.fori_loop(0, groups, issue, 0)


def wait_group(tiles_ref, buffer, sems, group):
    pltpu.make_async_copy(
        tiles_ref.at[pl.ds(0, GROUP)],
        buffer.at[pl.ds(group * GROUP, GROUP)],
        sems.at[group],
    ).wait()


def place(index):
    return pl.ds(pl.multiple_of(index * EDGE, EDGE), EDGE)


BATCH = 4


def forward_sum(part, list_ref, number_ref, pieces, tiles_ref, xbuf, tbuf, acc, xsem, tsem, start):
    groups = groups_of(number_ref, part)
    copies = [
        pltpu.make_async_copy(piece, xbuf.at[pl.ds(k * 1024, 1024)], xsem.at[k])
        for k, piece in enumerate(pieces)
    ]
    for copy in copies:
        copy.start()
    start_tiles(list_ref, tiles_ref, tbuf, tsem, part, groups, 0)
    start()
    xbuf[pl.ds(64 * EDGE, EDGE), :] = jnp.zeros((EDGE, EDGE), BF)
    for copy in copies:
        copy.wait()

    def body(group, carry):
        wait_group(tiles_ref, tbuf, tsem, group)
        for first in range(0, GROUP, BATCH):
            entries = [
                list_ref[part * SLOTS + group * GROUP + first + k] for k in range(BATCH)
            ]
            products = [
                jnp.dot(
                    tbuf[group * GROUP + first + k],
                    xbuf[place((entry >> 9) & 127), :],
                    preferred_element_type=F32,
                )
                for k, entry in enumerate(entries)
            ]
            for entry, product in zip(entries, products):
                acc[place(entry >> 16), :] += product
        return carry

    lax.fori_loop(0, groups, body, 0)


def over_tiles(count, step):
    def one(index, carry):
        step(place(index))
        return carry

    lax.fori_loop(0, count, one, 0)


def forward_send_kernel(part, list_ref, number_ref, *refs):
    pieces, (tiles_ref, out_ref, xbuf, tbuf, acc, xsem, tsem) = refs[:8], refs[8:]

    def start():
        def clear(at):
            acc[at, :] = jnp.zeros((EDGE, EDGE), F32)

        over_tiles(AREAS[part], clear)

    forward_sum(2 * part + 1, list_ref, number_ref, pieces, tiles_ref, xbuf, tbuf, acc, xsem, tsem, start)

    def store(at):
        out_ref[at, :] = acc[at, :].astype(BF)

    over_tiles(AREAS[part], store)


def forward_keep_kernel(part, list_ref, number_ref, *refs):
    pieces, refs = refs[:8], refs[8:]
    tiles_ref, got_ref, own, to_right, to_left, rest_right, rest_left, xbuf, tbuf, acc, xsem, tsem = refs

    def start():
        def load(at):
            acc[at, :] = got_ref[at, :].astype(F32)

        over_tiles(AREAS[part], load)

    forward_sum(2 * part, list_ref, number_ref, pieces, tiles_ref, xbuf, tbuf, acc, xsem, tsem, start)
    split_relay(lambda k, rows: acc[pl.ds(k, rows), :], own, to_right, to_left, rest_right, rest_left)


def split_relay(read, own, to_right, to_left, rest_right, rest_left):
    block = own.shape[0]
    half = block // 2
    for k in range(0, half, 64):
        at, low = pl.ds(k, 64), pl.ds(half + k, 64)
        own[at, :] = read(k, 64)
        own[low, :] = read(half + k, 64)
        to_right[at, :] = read(2 * block + k, 64).astype(BF)
        to_right[low, :] = read(block + half + k, 64).astype(BF)
        to_left[at, :] = read(2 * block + half + k, 64).astype(BF)
        to_left[low, :] = read(3 * block + k, 64).astype(BF)
        rest_right[at, :] = read(block + k, 64)
        rest_left[at, :] = read(3 * block + half + k, 64)


def split_direct(read, own, first, second, third):
    block = own.shape[0]
    for n, target in enumerate((own, first, second, third)):
        for k in range(0, block, 64):
            target[pl.ds(k, 64), :] = read(n * block + k, 64).astype(target.dtype)


def direct_shapes(block):
    return (shape_of(block, F32),) + (shape_of(block, BF),) * 3


def relay_shapes(block):
    half = block // 2
    return (shape_of(block, F32),) + (shape_of(block, BF),) * 2 + (shape_of(half, F32),) * 2


def forward_scratch(part):
    return [
        pltpu.VMEM((65 * EDGE, EDGE), BF),
        pltpu.VMEM((SLOTS, EDGE, EDGE), BF),
        pltpu.VMEM((AREAS[part] * EDGE, EDGE), F32),
        pltpu.SemaphoreType.DMA((8,)),
        pltpu.SemaphoreType.DMA((SLOTS // GROUP,)),
    ]


def forward_send(part, lists, numbers, pieces, tiles):
    return pl.pallas_call(
        functools.partial(forward_send_kernel, part),
        out_shape=shape_of(AREAS[part] * EDGE, BF),
        in_specs=[in_smem()] * 2 + [in_any()] * 9,
        out_specs=in_vmem(),
        scratch_shapes=forward_scratch(part),
        compiler_params=params(),
        name="forward_send",
    )(lists, numbers, *pieces, tiles)


def forward_keep(part, lists, numbers, pieces, tiles, got):
    return pl.pallas_call(
        functools.partial(forward_keep_kernel, part),
        out_shape=relay_shapes(AREAS[part] * EDGE // 4),
        in_specs=[in_smem()] * 2 + [in_any()] * 9 + [in_vmem()],
        out_specs=(in_vmem(),) * 5,
        scratch_shapes=forward_scratch(part),
        compiler_params=params(),
        name="forward_keep",
    )(lists, numbers, *pieces, tiles, got)


def direct_total(own, got):
    def read(k, rows):
        at = pl.ds(k, rows)
        total = own[at, :]
        for piece in got:
            total += piece[at, :].astype(F32)
        return total

    return read


def relay_total(own, from_left, from_right, late_left, late_right):
    half = late_left.shape[0]

    def read(k, rows):
        at = pl.ds(k, rows)
        if k < half:
            return own[at, :] + from_right[pl.ds(half + k, rows), :].astype(F32) + late_left[at, :].astype(F32)
        return own[at, :] + from_left[at, :].astype(F32) + late_right[pl.ds(k - half, rows), :].astype(F32)

    return read


def middle_kernel(rest_right, rest_left, from_left, from_right, on_right, on_left):
    half = rest_right.shape[0]
    on_right[...] = (rest_right[...] + from_left[pl.ds(0, half), :].astype(F32)).astype(BF)
    on_left[...] = (rest_left[...] + from_right[pl.ds(0, half), :].astype(F32)).astype(BF)


def relay_middle(rest_right, rest_left, from_left, from_right):
    return pl.pallas_call(
        middle_kernel,
        out_shape=(shape_of(rest_right.shape[0], BF),) * 2,
        in_specs=[in_vmem()] * 4,
        out_specs=(in_vmem(),) * 2,
        compiler_params=params(),
        name="middle",
    )(rest_right, rest_left, from_left, from_right)


def turn_kernel(*refs):
    split_direct(relay_total(*refs[:5]), *refs[5:])


def ring_turn(*values):
    return pl.pallas_call(
        turn_kernel,
        out_shape=direct_shapes(values[0].shape[0] // 4),
        in_specs=[in_vmem()] * 5,
        out_specs=(in_vmem(),) * 4,
        compiler_params=params(),
        name="turn",
    )(*values)


def join_kernel(count, *refs):
    pieces, out_ref = refs[:count], refs[count]
    at = 0
    for piece in pieces:
        out_ref[pl.ds(at, piece.shape[0]), :] = piece[...]
        at += piece.shape[0]


def join(pieces):
    return pl.pallas_call(
        functools.partial(join_kernel, len(pieces)),
        out_shape=shape_of(sum(p.shape[0] for p in pieces), BF),
        in_specs=[in_vmem()] * len(pieces),
        out_specs=in_vmem(),
        compiler_params=params(),
        name="join",
    )(*pieces)


def dense_kernel(chunk, *refs):
    sums, (weight_ref, bias_ref, cot_ref), outs = refs[:4], refs[4:7], refs[7:]
    rows = PARTS[chunk] * EDGE
    skip = chunk * PARTS[0] * EDGE
    hidden = direct_total(sums[0], sums[1:])(0, rows).astype(BF)
    weight = weight_ref[...]
    pre = jnp.dot(hidden, weight, preferred_element_type=F32) + bias_ref[...]
    sigma = jax.nn.sigmoid(pre)
    act = (pre * sigma).astype(BF)
    grad_pre = cot_ref[pl.ds(skip, rows), :].astype(F32) * sigma * (1.0 + pre * (1.0 - sigma))
    grad_round = grad_pre.astype(BF)
    weight_term = lax.dot_general(hidden, grad_round, (((0,), (0,)), ((), ())), preferred_element_type=F32)
    bias_term = jnp.broadcast_to(jnp.sum(grad_pre, axis=0, keepdims=True), (16, EDGE))
    if chunk:
        act_in, terms_in, act_ref, block_ref = outs
        act_ref[pl.ds(0, skip), :] = act_in[...]
        act_ref[pl.ds(skip, rows), :] = act
        block_ref[pl.ds(rows, EDGE), :] = (terms_in[pl.ds(0, EDGE), :] + weight_term).astype(BF)
        block_ref[pl.ds(rows + EDGE, 16), :] = (terms_in[pl.ds(EDGE, 16), :] + bias_term).astype(BF)
    else:
        act_ref, block_ref, terms_ref = outs
        act_ref[...] = act
        terms_ref[pl.ds(0, EDGE), :] = weight_term
        terms_ref[pl.ds(EDGE, 16), :] = bias_term
    for tile in range(PARTS[chunk]):
        part = grad_round[tile * EDGE : (tile + 1) * EDGE, :]
        back = lax.dot_general(weight, part, (((1,), (1,)), ((), ())), preferred_element_type=F32)
        block_ref[pl.ds(tile * EDGE, EDGE), :] = back.astype(BF)


def dense(chunk, sums, weight, bias, cotangent, before):
    rows = PARTS[chunk] * EDGE
    outs = (shape_of(sum(PARTS[: chunk + 1]) * EDGE, BF),)
    outs += (shape_of(BLOCK, BF),) if chunk else (shape_of(rows, BF), shape_of(TERMS, F32))
    return pl.pallas_call(
        functools.partial(dense_kernel, chunk),
        out_shape=outs,
        in_specs=[in_vmem()] * (7 + len(before)),
        out_specs=(in_vmem(),) * len(outs),
        compiler_params=params(),
        name="dense",
    )(*sums, weight, bias, cotangent, *before)


def backward_kernel(chunk, sizes, list_ref, backs_ref, number_ref, *refs):
    count = len(sizes)
    sources, tiles_ref = refs[:count], refs[count]
    out_ref, gbuf, tbuf, acc, gsem, tsem, bsem = refs[-7:]
    parts = (2 * chunk, 2 * chunk + 1)
    groups = [groups_of(number_ref, part) for part in parts]
    copies, at = [], 0
    for k, size in enumerate(sizes):
        copies.append(pltpu.make_async_copy(sources[k], gbuf.at[pl.ds(at, size)], gsem.at[k]))
        at += size
    if chunk:
        copies.append(pltpu.make_async_copy(refs[count + 1], acc.at[pl.ds(0, 64 * EDGE)], bsem.at[0]))
    for copy in copies:
        copy.start()
    start_tiles(list_ref, tiles_ref, tbuf, tsem, parts[0], groups[0], 0)
    start_tiles(list_ref, tiles_ref, tbuf, tsem, parts[1], groups[1], groups[0])

    def clear(at):
        acc[at, :] = jnp.zeros((EDGE, EDGE), F32)

    if chunk:
        clear(pl.ds(64 * EDGE, EDGE))
    else:
        over_tiles(65, clear)
    for copy in copies:
        copy.wait()
    for which, part in enumerate(parts):
        first_group = groups[0] * which

        def body(group, carry):
            wait_group(tiles_ref, tbuf, tsem, first_group + group)
            for first in range(0, GROUP, BATCH):
                entries = [backs_ref[part * SLOTS + group * GROUP + first + k] for k in range(BATCH)]
                products = [
                    jnp.dot(
                        gbuf[pl.ds(pl.multiple_of((entry >> 7) * 16, 16), EDGE), :],
                        tbuf[(first_group + group) * GROUP + first + k],
                        preferred_element_type=F32,
                    )
                    for k, entry in enumerate(entries)
                ]
                for entry, product in zip(entries, products):
                    acc[place(entry & 127), :] += product
            return carry

        lax.fori_loop(0, groups[which], body, 0)

    if not chunk:

        def store(at):
            out_ref[at, :] = acc[at, :]

        over_tiles(64, store)
        return
    for k in range(0, TERMS, 48):
        terms = jnp.zeros((48, EDGE), F32)
        for owner in range(NY * NZH * NCO):
            terms += gbuf[pl.ds(owner * BLOCK + PARTS[1] * EDGE + k, 48), :].astype(F32)
        for owner in range(8):
            out_ref[pl.ds(owner * SENT + 8 * EDGE + k, 48), :] = terms.astype(BF)
    for owner in range(8):
        for tile in range(8):
            at = pl.ds(owner * SENT + tile * EDGE, EDGE)
            out_ref[at, :] = acc[pl.ds((owner * 8 + tile) * EDGE, EDGE), :].astype(BF)


def backward(chunk, lists, backs, numbers, sources, tiles, before):
    sizes = tuple(source.shape[0] for source in sources)
    return pl.pallas_call(
        functools.partial(backward_kernel, chunk, sizes),
        out_shape=shape_of(8 * SENT, BF) if chunk else shape_of(64 * EDGE, F32),
        in_specs=[in_smem()] * 3 + [in_any()] * (len(sizes) + 1 + len(before)),
        out_specs=in_vmem(),
        scratch_shapes=[
            pltpu.VMEM((sum(sizes), EDGE), BF),
            pltpu.VMEM((SLOTS + GROUP, EDGE, EDGE), BF),
            pltpu.VMEM((65 * EDGE, EDGE), F32),
            pltpu.SemaphoreType.DMA((len(sizes),)),
            pltpu.SemaphoreType.DMA((SLOTS // GROUP + 1,)),
            pltpu.SemaphoreType.DMA((1,)),
        ],
        compiler_params=params(),
        name="backward",
    )(lists, backs, numbers, *sources, tiles, *before)


def last_kernel(got_ref, out_ref, weight_ref, bias_ref):
    for tile in range(8):
        total = jnp.zeros((EDGE, EDGE), F32)
        for peer in range(8):
            total += got_ref[pl.ds(peer * SENT + tile * EDGE, EDGE), :].astype(F32)
        out_ref[pl.ds(tile * EDGE, EDGE), :] = total.T.astype(BF)
    terms = jnp.zeros((TERMS, EDGE), F32)
    for peer in range(8):
        terms += got_ref[pl.ds(peer * SENT + 8 * EDGE, TERMS), :].astype(F32)
    weight_ref[...] = terms[:EDGE]
    bias_ref[...] = terms[EDGE : EDGE + 1]


def last(got):
    return pl.pallas_call(
        last_kernel,
        out_shape=(shape_of(8 * EDGE, BF), shape_of(EDGE, F32), shape_of(1, F32)),
        in_specs=[in_vmem()],
        out_specs=(in_vmem(),) * 3,
        compiler_params=params(),
        name="last",
    )(got)


def after(value, *others):
    return lax.optimization_barrier((value, *others))[0]


def around(block, axis):
    half = block.shape[0] // 2
    left, right = send_col(block, **{axis: 1}), send_col(block, **{axis: -1})
    return right, send_col(left[:half], **{axis: 1}), send_col(right[half:], **{axis: -1}), left


def on_device(features, tiles, tile_rows, tile_cols, tile_count, weight, bias, cotangent):
    tile_set = tiles[0, 0]
    part, entry, back = slot_entries(tile_rows[0, 0], tile_cols[0, 0])

    mine = features
    beside = after(send_row(mine, dzl=1), entry)
    mine_left, mine_right = send_row(mine, dx=1), send_row(mine, dx=-1)
    beside_left, beside_right = send_row(beside, dx=1), send_row(beside, dx=-1)
    mine_far = send_row(mine_left, dx=1)
    beside_far = send_row(beside_right, dx=-1)
    pieces = (mine, beside, mine_right, beside_right, mine_far, beside_far, mine_left, beside_left)
    lists, backs, numbers = make_bins(after(tile_count, mine_left, beside_right), part, entry, back)

    latest = []

    def gate(value):
        return after(value, *latest) if latest else value

    def ran(values):
        latest[:] = [values[0]]
        return values

    both = (0, 1)
    got = []
    for c in both:
        (part,) = ran([forward_send(c, gate(lists), numbers, pieces, tile_set)])
        got.append(send_col(part, dco=1))
    rings = []
    for c in both:
        rings.append(ran(forward_keep(c, gate(lists), numbers, pieces, tile_set, got[c])))
    bias_row = bias.reshape(1, EDGE)
    early = [(send_col(r[1], dy=1), send_col(r[2], dy=-1)) for r in rings]
    late = []
    for c in both:
        on_right, on_left = ran(relay_middle(gate(rings[c][3]), rings[c][4], *early[c]))
        late.append((send_col(on_right, dy=1), send_col(on_left, dy=-1)))
    sums = []
    for c in both:
        own, *blocks = ran(ring_turn(gate(rings[c][0]), *early[c], *late[c]))
        sums.append((own,) + tuple(send_col(block, dzh=n) for n, block in zip((1, 2, 3), blocks)))
    before, blocks = (), []
    for c in both:
        own, *others = sums[c]
        act, block, *terms = ran(dense(c, (gate(own), *others), weight, bias_row, cotangent, before))
        before = (act, *terms)
        blocks.append(block)

    gathered = lax.all_gather(blocks[1], "col", axis=0, tiled=True)
    joined = join((gate(blocks[0]),) + around(blocks[0], "dzh"))
    sources = (joined,) + around(joined, "dy")
    sources += tuple(send_col(source, dco=1) for source in sources)
    partial = backward(0, lists, backs, numbers, sources, tile_set, ())
    partial = backward(1, lists, backs, numbers, (gathered,), tile_set, (partial,))
    got = lax.all_to_all(partial.reshape(8, SENT, EDGE), "row", 0, 0, tiled=True)
    grad_features, grad_weight, grad_bias = last(got.reshape(8 * SENT, EDGE))
    return act, grad_features, grad_weight, grad_bias.reshape(EDGE)


def solution(mesh):
    placed = (
        P(("row", "col"), None),
        P("row", "col", None, None, None),
        P("row", "col", None),
        P("row", "col", None),
        P("row", "col"),
        P(),
        P(),
        P(("row", "col"), None),
    )
    return jax.shard_map(
        on_device,
        mesh=mesh,
        in_specs=placed,
        out_specs=(P(("row", "col"), None), P(("row", "col"), None), P(), P()),
        check_vma=False,
    )
```

```python
import functools

import jax
import jax.numpy as jnp
from jax import lax
from jax.experimental import pallas as pl
from jax.experimental.pallas import tpu as pltpu
from jax.sharding import PartitionSpec as P

NX, NZL, NY, NZH, NCO = 4, 2, 4, 4, 2
EDGE = 128
PARTS = (4, 4)
AREAS = tuple(NY * NZH * tiles for tiles in PARTS)
TERMS = EDGE + 16
BLOCK = PARTS[1] * EDGE + TERMS
SENT = 8 * EDGE + TERMS
GROUP = 8
SLOTS = 384
VMEM = 64 * 1024 * 1024 - 64 * 1024
BF = jnp.bfloat16
F32 = jnp.float32


def moved(index, count, step):
    return (index + step) % count


def row_perm(dx=0, dzl=0):
    return [
        (x * NZL + z, moved(x, NX, dx) * NZL + moved(z, NZL, dzl))
        for x in range(NX)
        for z in range(NZL)
    ]


def col_perm(dy=0, dzh=0, dco=0):
    return [
        (
            (y * NZH + z) * NCO + c,
            (moved(y, NY, dy) * NZH + moved(z, NZH, dzh)) * NCO + moved(c, NCO, dco),
        )
        for y in range(NY)
        for z in range(NZH)
        for c in range(NCO)
    ]


def send_row(value, **step):
    return lax.ppermute(value, "row", row_perm(**step))


def send_col(value, **step):
    return lax.ppermute(value, "col", col_perm(**step))


def in_smem():
    return pl.BlockSpec(memory_space=pltpu.SMEM)


def in_vmem():
    return pl.BlockSpec(memory_space=pltpu.VMEM)


def in_any():
    return pl.BlockSpec(memory_space=pl.ANY)


def shape_of(rows, dtype):
    return jax.ShapeDtypeStruct((rows, EDGE), dtype)


def params():
    return pltpu.CompilerParams(vmem_limit_bytes=VMEM)


def slot_entries(row_tiles, col_tiles):
    row, col = lax.axis_index("row"), lax.axis_index("col")
    my_x, my_zl = row >> 1, row & 1
    my_y, my_zh, my_co = col >> 3, (col >> 1) & 3, col & 1
    owner, inner = row_tiles >> 3, row_tiles & 7
    dy = ((owner >> 3) - my_y) & 3
    dz = (((owner >> 1) & 3) - my_zh) & 3
    other = (owner & 1) ^ my_co
    later = inner >= PARTS[0]
    part = later.astype(jnp.int32) * 2 + other
    ring = dy * NZH + dz
    row_place = jnp.where(later, ring * PARTS[1] + inner - PARTS[0], ring * PARTS[0] + inner)
    source = jnp.where(
        later,
        owner * (BLOCK // 16) + (inner - PARTS[0]) * (EDGE // 16),
        (other * AREAS[0] + row_place) * (EDGE // 16),
    )
    backward = col_tiles | (source << 7)
    owner, inner = col_tiles >> 3, col_tiles & 7
    dx = ((owner >> 1) - my_x) & 3
    col_place = (dx * 2 + ((owner & 1) ^ my_zl)) * 8 + inner
    slot = lax.broadcasted_iota(jnp.int32, row_tiles.shape, row_tiles.ndim - 1)
    return part, slot | (col_place << 9) | (row_place << 16), backward


def bins_kernel(count_ref, part_ref, entry_ref, back_ref, list_ref, backs_ref, number_ref):
    for part in range(4):
        number_ref[part] = 0

    def one(slot, carry):
        part = part_ref[slot]
        at = number_ref[part]
        list_ref[part * SLOTS + at] = entry_ref[slot]
        backs_ref[part * SLOTS + at] = back_ref[slot]
        number_ref[part] = at + 1
        return carry

    lax.fori_loop(0, count_ref[0, 0], one, 0)
    for part in range(4):
        last = number_ref[part]
        for extra in range(GROUP - 1):
            list_ref[part * SLOTS + last + extra] = 64 << 9
            backs_ref[part * SLOTS + last + extra] = 64


def make_bins(count, part, entry, back):
    return pl.pallas_call(
        bins_kernel,
        out_shape=(
            jax.ShapeDtypeStruct((4 * SLOTS,), jnp.int32),
            jax.ShapeDtypeStruct((4 * SLOTS,), jnp.int32),
            jax.ShapeDtypeStruct((4,), jnp.int32),
        ),
        in_specs=[in_smem()] * 4,
        out_specs=(in_smem(),) * 3,
        compiler_params=params(),
        name="bins",
    )(count, part, entry, back)


def groups_of(number_ref, part):
    return (number_ref[part] + (GROUP - 1)) // GROUP


def start_tiles(list_ref, tiles_ref, buffer, sems, part, groups, first_group):
    def issue(group, carry):
        for k in range(GROUP):
            entry = list_ref[part * SLOTS + group * GROUP + k]
            pltpu.make_async_copy(
                tiles_ref.at[entry & 511],
                buffer.at[(first_group + group) * GROUP + k],
                sems.at[first_group + group],
            ).start()
        return carry

    lax.fori_loop(0, groups, issue, 0)


def wait_group(tiles_ref, buffer, sems, group):
    pltpu.make_async_copy(
        tiles_ref.at[pl.ds(0, GROUP)],
        buffer.at[pl.ds(group * GROUP, GROUP)],
        sems.at[group],
    ).wait()


def place(index):
    return pl.ds(pl.multiple_of(index * EDGE, EDGE), EDGE)


BATCH = 4


def forward_sum(part, list_ref, number_ref, pieces, tiles_ref, xbuf, tbuf, acc, xsem, tsem, start):
    groups = groups_of(number_ref, part)
    copies = [
        pltpu.make_async_copy(piece, xbuf.at[pl.ds(k * 1024, 1024)], xsem.at[k])
        for k, piece in enumerate(pieces)
    ]
    for copy in copies:
        copy.start()
    start_tiles(list_ref, tiles_ref, tbuf, tsem, part, groups, 0)
    start()
    xbuf[pl.ds(64 * EDGE, EDGE), :] = jnp.zeros((EDGE, EDGE), BF)
    for copy in copies:
        copy.wait()

    def body(group, carry):
        wait_group(tiles_ref, tbuf, tsem, group)
        for first in range(0, GROUP, BATCH):
            entries = [
                list_ref[part * SLOTS + group * GROUP + first + k] for k in range(BATCH)
            ]
            products = [
                jnp.dot(
                    tbuf[group * GROUP + first + k],
                    xbuf[place((entry >> 9) & 127), :],
                    preferred_element_type=F32,
                )
                for k, entry in enumerate(entries)
            ]
            for entry, product in zip(entries, products):
                acc[place(entry >> 16), :] += product
        return carry

    lax.fori_loop(0, groups, body, 0)


def over_tiles(count, step):
    def one(index, carry):
        step(place(index))
        return carry

    lax.fori_loop(0, count, one, 0)


def forward_send_kernel(part, list_ref, number_ref, *refs):
    pieces, (tiles_ref, out_ref, xbuf, tbuf, acc, xsem, tsem) = refs[:8], refs[8:]

    def start():
        def clear(at):
            acc[at, :] = jnp.zeros((EDGE, EDGE), F32)

        over_tiles(AREAS[part], clear)

    forward_sum(2 * part + 1, list_ref, number_ref, pieces, tiles_ref, xbuf, tbuf, acc, xsem, tsem, start)

    def store(at):
        out_ref[at, :] = acc[at, :].astype(BF)

    over_tiles(AREAS[part], store)


def forward_keep_kernel(part, list_ref, number_ref, *refs):
    pieces, refs = refs[:8], refs[8:]
    tiles_ref, got_ref, outs = refs[0], refs[1], refs[2:-5]
    xbuf, tbuf, acc, xsem, tsem = refs[-5:]

    def start():
        def load(at):
            acc[at, :] = got_ref[at, :].astype(F32)

        over_tiles(AREAS[part], load)

    forward_sum(2 * part, list_ref, number_ref, pieces, tiles_ref, xbuf, tbuf, acc, xsem, tsem, start)
    split = split_direct if part else split_relay
    split(lambda k, rows: acc[pl.ds(k, rows), :], *outs)


def split_relay(read, own, to_right, to_left, rest_right, rest_left):
    block = own.shape[0]
    half = block // 2
    for k in range(0, half, 64):
        at, low = pl.ds(k, 64), pl.ds(half + k, 64)
        own[at, :] = read(k, 64)
        own[low, :] = read(half + k, 64)
        to_right[at, :] = read(2 * block + k, 64).astype(BF)
        to_right[low, :] = read(block + half + k, 64).astype(BF)
        to_left[at, :] = read(2 * block + half + k, 64).astype(BF)
        to_left[low, :] = read(3 * block + k, 64).astype(BF)
        rest_right[at, :] = read(block + k, 64)
        rest_left[at, :] = read(3 * block + half + k, 64)


def split_direct(read, own, first, second, third):
    block = own.shape[0]
    for n, target in enumerate((own, first, second, third)):
        for k in range(0, block, 64):
            target[pl.ds(k, 64), :] = read(n * block + k, 64).astype(target.dtype)


def direct_shapes(block):
    return (shape_of(block, F32),) + (shape_of(block, BF),) * 3


def relay_shapes(block):
    half = block // 2
    return (shape_of(block, F32),) + (shape_of(block, BF),) * 2 + (shape_of(half, F32),) * 2


def forward_scratch(part):
    return [
        pltpu.VMEM((65 * EDGE, EDGE), BF),
        pltpu.VMEM((SLOTS, EDGE, EDGE), BF),
        pltpu.VMEM((AREAS[part] * EDGE, EDGE), F32),
        pltpu.SemaphoreType.DMA((8,)),
        pltpu.SemaphoreType.DMA((SLOTS // GROUP,)),
    ]


def forward_send(part, lists, numbers, pieces, tiles):
    return pl.pallas_call(
        functools.partial(forward_send_kernel, part),
        out_shape=shape_of(AREAS[part] * EDGE, BF),
        in_specs=[in_smem()] * 2 + [in_any()] * 9,
        out_specs=in_vmem(),
        scratch_shapes=forward_scratch(part),
        compiler_params=params(),
        name="forward_send",
    )(lists, numbers, *pieces, tiles)


def forward_keep(part, lists, numbers, pieces, tiles, got):
    return pl.pallas_call(
        functools.partial(forward_keep_kernel, part),
        out_shape=(direct_shapes if part else relay_shapes)(AREAS[part] * EDGE // 4),
        in_specs=[in_smem()] * 2 + [in_any()] * 9 + [in_vmem()],
        out_specs=(in_vmem(),) * (4 if part else 5),
        scratch_shapes=forward_scratch(part),
        compiler_params=params(),
        name="forward_keep",
    )(lists, numbers, *pieces, tiles, got)


def direct_total(own, got):
    def read(k, rows):
        at = pl.ds(k, rows)
        total = own[at, :]
        for piece in got:
            total += piece[at, :].astype(F32)
        return total

    return read


def relay_total(own, from_left, from_right, late_left, late_right):
    half = late_left.shape[0]

    def read(k, rows):
        at = pl.ds(k, rows)
        if k < half:
            return own[at, :] + from_right[pl.ds(half + k, rows), :].astype(F32) + late_left[at, :].astype(F32)
        return own[at, :] + from_left[at, :].astype(F32) + late_right[pl.ds(k - half, rows), :].astype(F32)

    return read


def middle_kernel(rest_right, rest_left, from_left, from_right, on_right, on_left):
    half = rest_right.shape[0]
    on_right[...] = (rest_right[...] + from_left[pl.ds(0, half), :].astype(F32)).astype(BF)
    on_left[...] = (rest_left[...] + from_right[pl.ds(0, half), :].astype(F32)).astype(BF)


def relay_middle(rest_right, rest_left, from_left, from_right):
    return pl.pallas_call(
        middle_kernel,
        out_shape=(shape_of(rest_right.shape[0], BF),) * 2,
        in_specs=[in_vmem()] * 4,
        out_specs=(in_vmem(),) * 2,
        compiler_params=params(),
        name="middle",
    )(rest_right, rest_left, from_left, from_right)


def turn_kernel(*refs):
    values, outs = refs[:-4], refs[-4:]
    read = relay_total(*values) if len(values) == 5 else direct_total(values[0], values[1:])
    split_direct(read, *outs)


def ring_turn(*values):
    return pl.pallas_call(
        turn_kernel,
        out_shape=direct_shapes(values[0].shape[0] // 4),
        in_specs=[in_vmem()] * len(values),
        out_specs=(in_vmem(),) * 4,
        compiler_params=params(),
        name="turn",
    )(*values)


def join_kernel(count, *refs):
    pieces, out_ref = refs[:count], refs[count]
    at = 0
    for piece in pieces:
        out_ref[pl.ds(at, piece.shape[0]), :] = piece[...]
        at += piece.shape[0]


def join(pieces):
    return pl.pallas_call(
        functools.partial(join_kernel, len(pieces)),
        out_shape=shape_of(sum(p.shape[0] for p in pieces), BF),
        in_specs=[in_vmem()] * len(pieces),
        out_specs=in_vmem(),
        compiler_params=params(),
        name="join",
    )(*pieces)


def dense_kernel(chunk, *refs):
    sums, (weight_ref, bias_ref, cot_ref), outs = refs[:4], refs[4:7], refs[7:]
    rows = PARTS[chunk] * EDGE
    skip = chunk * PARTS[0] * EDGE
    hidden = direct_total(sums[0], sums[1:])(0, rows).astype(BF)
    weight = weight_ref[...]
    pre = jnp.dot(hidden, weight, preferred_element_type=F32) + bias_ref[...]
    sigma = jax.nn.sigmoid(pre)
    act = (pre * sigma).astype(BF)
    grad_pre = cot_ref[pl.ds(skip, rows), :].astype(F32) * sigma * (1.0 + pre * (1.0 - sigma))
    grad_round = grad_pre.astype(BF)
    weight_term = lax.dot_general(hidden, grad_round, (((0,), (0,)), ((), ())), preferred_element_type=F32)
    bias_term = jnp.broadcast_to(jnp.sum(grad_pre, axis=0, keepdims=True), (16, EDGE))
    if chunk:
        act_in, terms_in, act_ref, block_ref = outs
        act_ref[pl.ds(0, skip), :] = act_in[...]
        act_ref[pl.ds(skip, rows), :] = act
        block_ref[pl.ds(rows, EDGE), :] = (terms_in[pl.ds(0, EDGE), :] + weight_term).astype(BF)
        block_ref[pl.ds(rows + EDGE, 16), :] = (terms_in[pl.ds(EDGE, 16), :] + bias_term).astype(BF)
    else:
        act_ref, block_ref, terms_ref = outs
        act_ref[...] = act
        terms_ref[pl.ds(0, EDGE), :] = weight_term
        terms_ref[pl.ds(EDGE, 16), :] = bias_term
    for tile in range(PARTS[chunk]):
        part = grad_round[tile * EDGE : (tile + 1) * EDGE, :]
        back = lax.dot_general(weight, part, (((1,), (1,)), ((), ())), preferred_element_type=F32)
        block_ref[pl.ds(tile * EDGE, EDGE), :] = back.astype(BF)


def dense(chunk, sums, weight, bias, cotangent, before):
    rows = PARTS[chunk] * EDGE
    outs = (shape_of(sum(PARTS[: chunk + 1]) * EDGE, BF),)
    outs += (shape_of(BLOCK, BF),) if chunk else (shape_of(rows, BF), shape_of(TERMS, F32))
    return pl.pallas_call(
        functools.partial(dense_kernel, chunk),
        out_shape=outs,
        in_specs=[in_vmem()] * (7 + len(before)),
        out_specs=(in_vmem(),) * len(outs),
        compiler_params=params(),
        name="dense",
    )(*sums, weight, bias, cotangent, *before)


def backward_kernel(chunk, sizes, list_ref, backs_ref, number_ref, *refs):
    count = len(sizes)
    sources, tiles_ref = refs[:count], refs[count]
    out_ref, gbuf, tbuf, acc, gsem, tsem, bsem = refs[-7:]
    parts = (2 * chunk, 2 * chunk + 1)
    groups = [groups_of(number_ref, part) for part in parts]
    copies, at = [], 0
    for k, size in enumerate(sizes):
        copies.append(pltpu.make_async_copy(sources[k], gbuf.at[pl.ds(at, size)], gsem.at[k]))
        at += size
    if chunk:
        copies.append(pltpu.make_async_copy(refs[count + 1], acc.at[pl.ds(0, 64 * EDGE)], bsem.at[0]))
    for copy in copies:
        copy.start()
    start_tiles(list_ref, tiles_ref, tbuf, tsem, parts[0], groups[0], 0)
    start_tiles(list_ref, tiles_ref, tbuf, tsem, parts[1], groups[1], groups[0])

    def clear(at):
        acc[at, :] = jnp.zeros((EDGE, EDGE), F32)

    if chunk:
        clear(pl.ds(64 * EDGE, EDGE))
    else:
        over_tiles(65, clear)
    for copy in copies:
        copy.wait()
    for which, part in enumerate(parts):
        first_group = groups[0] * which

        def body(group, carry):
            wait_group(tiles_ref, tbuf, tsem, first_group + group)
            for first in range(0, GROUP, BATCH):
                entries = [backs_ref[part * SLOTS + group * GROUP + first + k] for k in range(BATCH)]
                products = [
                    jnp.dot(
                        gbuf[pl.ds(pl.multiple_of((entry >> 7) * 16, 16), EDGE), :],
                        tbuf[(first_group + group) * GROUP + first + k],
                        preferred_element_type=F32,
                    )
                    for k, entry in enumerate(entries)
                ]
                for entry, product in zip(entries, products):
                    acc[place(entry & 127), :] += product
            return carry

        lax.fori_loop(0, groups[which], body, 0)

    if not chunk:

        def store(at):
            out_ref[at, :] = acc[at, :]

        over_tiles(64, store)
        return
    for k in range(0, TERMS, 48):
        terms = jnp.zeros((48, EDGE), F32)
        for owner in range(NY * NZH * NCO):
            terms += gbuf[pl.ds(owner * BLOCK + PARTS[1] * EDGE + k, 48), :].astype(F32)
        for owner in range(8):
            out_ref[pl.ds(owner * SENT + 8 * EDGE + k, 48), :] = terms.astype(BF)
    for owner in range(8):
        for tile in range(8):
            at = pl.ds(owner * SENT + tile * EDGE, EDGE)
            out_ref[at, :] = acc[pl.ds((owner * 8 + tile) * EDGE, EDGE), :].astype(BF)


def backward(chunk, lists, backs, numbers, sources, tiles, before):
    sizes = tuple(source.shape[0] for source in sources)
    return pl.pallas_call(
        functools.partial(backward_kernel, chunk, sizes),
        out_shape=shape_of(8 * SENT, BF) if chunk else shape_of(64 * EDGE, F32),
        in_specs=[in_smem()] * 3 + [in_any()] * (len(sizes) + 1 + len(before)),
        out_specs=in_vmem(),
        scratch_shapes=[
            pltpu.VMEM((sum(sizes), EDGE), BF),
            pltpu.VMEM((SLOTS + GROUP, EDGE, EDGE), BF),
            pltpu.VMEM((65 * EDGE, EDGE), F32),
            pltpu.SemaphoreType.DMA((len(sizes),)),
            pltpu.SemaphoreType.DMA((SLOTS // GROUP + 1,)),
            pltpu.SemaphoreType.DMA((1,)),
        ],
        compiler_params=params(),
        name="backward",
    )(lists, backs, numbers, *sources, tiles, *before)


def last_kernel(got_ref, out_ref, weight_ref, bias_ref):
    for tile in range(8):
        total = jnp.zeros((EDGE, EDGE), F32)
        for peer in range(8):
            total += got_ref[pl.ds(peer * SENT + tile * EDGE, EDGE), :].astype(F32)
        out_ref[pl.ds(tile * EDGE, EDGE), :] = total.T.astype(BF)
    terms = jnp.zeros((TERMS, EDGE), F32)
    for peer in range(8):
        terms += got_ref[pl.ds(peer * SENT + 8 * EDGE, TERMS), :].astype(F32)
    weight_ref[...] = terms[:EDGE]
    bias_ref[...] = terms[EDGE : EDGE + 1]


def last(got):
    return pl.pallas_call(
        last_kernel,
        out_shape=(shape_of(8 * EDGE, BF), shape_of(EDGE, F32), shape_of(1, F32)),
        in_specs=[in_vmem()],
        out_specs=(in_vmem(),) * 3,
        compiler_params=params(),
        name="last",
    )(got)


def after(value, *others):
    return lax.optimization_barrier((value, *others))[0]


def around(block, axis):
    half = block.shape[0] // 2
    left, right = send_col(block, **{axis: 1}), send_col(block, **{axis: -1})
    return right, send_col(left[:half], **{axis: 1}), send_col(right[half:], **{axis: -1}), left


def on_device(features, tiles, tile_rows, tile_cols, tile_count, weight, bias, cotangent):
    tile_set = tiles[0, 0]
    part, entry, back = slot_entries(tile_rows[0, 0], tile_cols[0, 0])

    mine = features
    beside = after(send_row(mine, dzl=1), entry)
    mine_left, mine_right = send_row(mine, dx=1), send_row(mine, dx=-1)
    beside_left, beside_right = send_row(beside, dx=1), send_row(beside, dx=-1)
    mine_far = send_row(mine_left, dx=1)
    beside_far = send_row(beside_right, dx=-1)
    pieces = (mine, beside, mine_right, beside_right, mine_far, beside_far, mine_left, beside_left)
    lists, backs, numbers = make_bins(after(tile_count, mine_left, beside_right), part, entry, back)

    latest = []

    def gate(value):
        return after(value, *latest) if latest else value

    def ran(values):
        latest[:] = [values[0]]
        return values

    both = (0, 1)
    got = []
    for c in both:
        (part,) = ran([forward_send(c, gate(lists), numbers, pieces, tile_set)])
        got.append(send_col(part, dco=1))
    rings = []
    for c in both:
        rings.append(ran(forward_keep(c, gate(lists), numbers, pieces, tile_set, got[c])))
    bias_row = bias.reshape(1, EDGE)
    own, to_right, to_left, rest_right, rest_left = rings[0]
    early = (send_col(to_right, dy=1), send_col(to_left, dy=-1))
    straight = tuple(send_col(block, dy=n) for n, block in zip((1, 2, 3), rings[1][1:]))
    on_right, on_left = ran(relay_middle(gate(rest_right), rest_left, *early))
    late = (send_col(on_right, dy=1), send_col(on_left, dy=-1))
    sums = []
    for own, came in ((own, early + late), (rings[1][0], straight)):
        own, *blocks = ran(ring_turn(gate(own), *came))
        sums.append((own,) + tuple(send_col(block, dzh=n) for n, block in zip((1, 2, 3), blocks)))
    before, blocks = (), []
    for c in both:
        own, *others = sums[c]
        act, block, *terms = ran(dense(c, (gate(own), *others), weight, bias_row, cotangent, before))
        before = (act, *terms)
        blocks.append(block)

    gathered = lax.all_gather(blocks[1], "col", axis=0, tiled=True)
    joined = join((gate(blocks[0]),) + around(blocks[0], "dzh"))
    sources = (joined,) + around(joined, "dy")
    sources += tuple(send_col(source, dco=1) for source in sources)
    partial = backward(0, lists, backs, numbers, sources, tile_set, ())
    partial = backward(1, lists, backs, numbers, (gathered,), tile_set, (partial,))
    got = lax.all_to_all(partial.reshape(8, SENT, EDGE), "row", 0, 0, tiled=True)
    grad_features, grad_weight, grad_bias = last(got.reshape(8 * SENT, EDGE))
    return act, grad_features, grad_weight, grad_bias.reshape(EDGE)


def solution(mesh):
    placed = (
        P(("row", "col"), None),
        P("row", "col", None, None, None),
        P("row", "col", None),
        P("row", "col", None),
        P("row", "col"),
        P(),
        P(),
        P(("row", "col"), None),
    )
    return jax.shard_map(
        on_device,
        mesh=mesh,
        in_specs=placed,
        out_specs=(P(("row", "col"), None), P(("row", "col"), None), P(), P()),
        check_vma=False,
    )
```
